128 devices in a mesh: seq: 8 (over x, core), grp: 16 (over z, y).
Axes of the slice: x: 4, y: 4, z: 4, core: 2. Of those that a mesh axis runs over, the one named last changes fastest.
Arguments:
- guess: float32 [2, 4096, 256], P(None, ('seq', 'grp')), may hold values from -24 to 24
- inputs: bfloat16 [2, 4096, 256], P(None, ('seq', 'grp')), may hold values from -6 to 6
- initial: float32 [2, 256], replicated, may hold values from -6 to 6
- skew_base: float32 [256, 256], replicated, may hold values from -0.09375 to 0.09375
- in_weight: bfloat16 [256, 256], replicated, may hold values from -0.375 to 0.375
- bias: float32 [256], replicated, may hold values from -3 to 3
- rate: float32 [256], replicated, may hold values from 2e-05 to 0.0001
Outputs:
- new_states: float32 [2, 4096, 256], P(None, ('seq', 'grp'))
The draws below stay inside these ranges and needn't reach their ends.
All inputs are finite; a program needn't handle non-finite values.
Results may differ from the reference program's by a relative error of at most 0.0003.
Values sent between devices are 32-bit elements; how exact they have to be, the bound alone decides.
A program may use at most 64 MiB of HBM per device.

```python
import math
import jax
import jax.numpy as jnp
from jax import lax

D = 256
SEQS = 2
TSTEPS = 4096


def steps_of(rng, shape, cuts, low, largest):
    factor_of = 1.0
    for position, parts in cuts:
        steps = jax.random.uniform(jax.random.fold_in(jax.random.fold_in(rng, 6), position), (parts,), jnp.float32, low / len(cuts), largest / len(cuts))
        factor_of = factor_of * jnp.repeat(jnp.exp(steps), shape[position] // parts).reshape((-1,) + (1,) * (len(shape) - 1 - position))
    return factor_of


def centred(key, dims, width, reach, shards=(), held_as=jnp.bfloat16):
    level = steps_of(key, dims, shards, -0.22, 0.18) if shards else 1.0
    values = jax.random.normal(key, dims, jnp.float32) * width * level
    return jnp.minimum(jnp.maximum(values, -reach), reach).astype(held_as)


def setup_inputs(seed: int = 0) -> dict:
    key_of = jax.random.split(jax.random.key(seed), 8)
    return {
        "guess": centred(key_of[0], (SEQS, TSTEPS, D), 4.0, 24.0, ((1, 128),), jnp.float32),
        "inputs": centred(key_of[1], (SEQS, TSTEPS, D), 1.0, 6.0, ((1, 128),)),
        "initial": centred(key_of[2], (SEQS, D), 1.0, 6.0, (), jnp.float32),
        "skew_base": centred(key_of[3], (D, D), (16 * D) ** -0.5, 0.09375, (), jnp.float32),
        "in_weight": centred(key_of[4], (D, D), D ** -0.5, 0.375),
        "bias": centred(key_of[5], (D,), 0.5, 3.0, (), jnp.float32),
        "rate": jnp.clip(jnp.exp(jax.random.uniform(key_of[6], (D,), jnp.float32, math.log(1.9999999494757503e-05), math.log(0.0001))), 1.9999999494757503e-05, 0.0001),
    }


step_gain = 0.05


def reference(guess, inputs, initial, skew_base, in_weight, bias, rate):
    highest = lax.Precision.HIGHEST
    skew = skew_base - skew_base.T
    prev = jnp.concatenate([initial[:, None, :], guess[:, :-1, :]], axis=1)
    lin = jnp.einsum('btd,ed->bte', prev, skew, precision=highest)
    pre = jnp.einsum('btd,de->bte', inputs.astype(jnp.float32), in_weight.astype(jnp.float32), precision=highest) + bias
    act = jnp.tanh(lin + pre)
    slope = 1.0 - act * act
    offset = step_gain * (act - slope * lin)
    keep = 1.0 - rate

    def advance(state, pieces):
        slope_now, offset_now = pieces
        turned = jnp.einsum('bd,ed->be', state, skew, precision=highest)
        state = keep * state + step_gain * slope_now * turned + offset_now
        return state, state

    final, states = lax.scan(advance, initial, (jnp.swapaxes(slope, 0, 1), jnp.swapaxes(offset, 0, 1)))
    return jnp.swapaxes(states, 0, 1)
```

```python
import jax
import jax.numpy as jnp
from jax import lax
from jax.experimental import pallas as pl
from jax.experimental.pallas import tpu as pltpu
from jax.sharding import PartitionSpec as P

SEQ_GRP = ("seq", "grp")
MESH = pl.DeviceIdType.MESH
F32 = jnp.float32
BF16 = jnp.bfloat16
GAIN = 0.05

WIDTH = 256
STEPS = 32
SUB = 8
SUBS = STEPS // SUB
ROWS = WIDTH + 16
SLAB_Z = 1


def split(value):
    high = value.astype(BF16)
    return high, (value - high.astype(F32)).astype(BF16)


def dot(a, b):
    return jnp.dot(a, b, preferred_element_type=F32)


def dot3(value, high, low):
    top, rest = split(value)
    return dot(top, high) + dot(top, low) + dot(rest, high)


def first_row(rows):
    return (lax.broadcasted_iota(jnp.int32, (rows, WIDTH), 0) == 0).astype(F32)


def as_columns(row):
    turned = jnp.transpose(jnp.broadcast_to(row, (128, WIDTH)))
    return jnp.concatenate([turned, turned], axis=1)


def applied(columns, matrix, vector):
    return jnp.sum(matrix * columns, axis=0, keepdims=True) + vector


def kernel(
    guess, inputs, initial, base, weight, bias, rate, out,
    skew_hi, skew_lo, before, prev, slope, offset, chain, ymaps, ywhole, gmaps, gwhole,
    xin, xout, gin, gout, fin, fout, state, slope2, offset2, out2,
    psem, ysend, yrecv, gsend, grecv, xsem, esend, erecv, fsend, frecv,
):
    seq_at, grp_at = lax.axis_index("seq"), lax.axis_index("grp")
    x, c = seq_at // 2, seq_at % 2
    z, y = grp_at // 4, grp_at % 4
    place = x * 32 + c * 16 + z * 4 + y

    def device(x, c, z, y):
        return (x * 2 + c, z * 4 + y)

    def block(index):
        return (index // 16, index % 16)

    mine = y // 2
    yroot = c == y % 2
    slab = yroot & (c == 0) & (z == SLAB_Z)
    root_at = [2 * s + c for s in range(2)]
    slab_id = device(x, 0, SLAB_Z, 2 * mine)

    barrier = pltpu.get_barrier_semaphore()

    def greet(target):
        pl.semaphore_signal(barrier, inc=1, device_id=target, device_id_type=MESH)

    @pl.when(place > 0)
    def _():
        greet(block(place - 1))

    for s in range(2):

        @pl.when(root_at[s] != y)
        def _():
            greet(device(x, c, z, root_at[s]))

    @pl.when(yroot)
    def _():
        for k in range(1, 4):
            greet(device(x, c, z, (y + k) % 4))

    @pl.when(yroot & jnp.logical_not(slab))
    def _():
        greet(slab_id)

    @pl.when(slab)
    def _():
        for k in range(8):
            if k != SLAB_Z:
                greet(device(x, k // 4, k % 4, 2 * mine + k // 4))

    @pl.when(slab & (x > 0))
    def _():
        greet(device(x - 1, c, z, y))

    skew_t = jnp.transpose(base[...]) - base[...]
    high, low = split(skew_t)
    skew_hi[...] = high
    skew_lo[...] = low
    keep = 1.0 - rate[...]
    pre = dot(inputs[...].reshape(2 * STEPS, WIDTH), weight[...]) + bias[...]
    for s in range(2):
        prev[s, 8 : 8 + STEPS, :] = guess[s]
    eye = (
        lax.broadcasted_iota(jnp.int32, (ROWS, WIDTH), 0)
        == lax.broadcasted_iota(jnp.int32, (ROWS, WIDTH), 1)
    ).astype(F32)
    for s in range(2):
        chain[0, s] = eye

    one = jnp.int32(1)
    none = jnp.int32(0)
    sends = jnp.where(place < 127, one, none) + jnp.where(yroot, one, one + one)
    sends = sends + jnp.where(yroot, one * 3, none) + jnp.where(yroot, one, none)
    sends = sends + jnp.where(slab, one * 6, none) + jnp.where(slab & (x < 3), one, none)
    pl.semaphore_wait(barrier, sends)

    ahead = jnp.minimum(place + 1, 127)
    tail = pltpu.make_async_remote_copy(
        src_ref=guess.at[:, STEPS - 8 :, :],
        dst_ref=before,
        send_sem=psem.at[0],
        recv_sem=psem.at[1],
        device_id=block(ahead),
        device_id_type=MESH,
    )

    @pl.when(place < 127)
    def _():
        tail.start()

    @pl.when(place > 0)
    def _():
        tail.wait_recv()
        for s in range(2):
            prev[s, 7:8, :] = before[s, 7:8, :]

    @pl.when(place == 0)
    def _():
        for s in range(2):
            prev[s, 7:8, :] = initial[s : s + 1, :]

    earlier = jnp.concatenate([prev[s, 7 : 7 + STEPS, :] for s in range(2)], axis=0)
    lin = dot3(earlier, skew_hi[...], skew_lo[...])
    act = jnp.tanh(lin + pre)
    steep = 1.0 - act * act
    slope[...] = GAIN * steep
    offset[...] = GAIN * (act - steep * lin)
    for half in range(2):
        lanes = slice(half * 128, half * 128 + 128)
        slope2[half] = slope[:, lanes]
        offset2[half] = offset[:, lanes]

    top = first_row(16)

    def sub_block(sub, carry):
        for inner in range(SUB):
            src = sub if inner == 0 else sub + 1
            for s in range(2):
                at = s * STEPS + sub * SUB + inner
                held = chain[src, s]
                turned = dot3(held, skew_hi[...], skew_lo[...])
                moved = keep * held + slope[pl.ds(at, 1), :] * turned
                chain[sub + 1, s, :WIDTH] = moved[:WIDTH]
                chain[sub + 1, s, WIDTH:] = moved[WIDTH:] + top * offset[pl.ds(at, 1), :]
        return carry

    lax.fori_loop(0, SUBS, sub_block, 0)

    to_root = []
    for s in range(2):
        copy = pltpu.make_async_remote_copy(
            src_ref=chain.at[SUBS, s],
            dst_ref=ymaps.at[y],
            send_sem=ysend.at[s],
            recv_sem=yrecv.at[y],
            device_id=device(x, c, z, root_at[s]),
            device_id_type=MESH,
        )
        to_root.append(copy)

        @pl.when(root_at[s] != y)
        def _():
            copy.start()

    def arrival(maps, sems, k):
        return pltpu.make_async_remote_copy(
            src_ref=maps.at[k],
            dst_ref=maps.at[k],
            send_sem=sems.at[k],
            recv_sem=sems.at[k],
            device_id=device(x, c, z, (y + 1) % 4),
            device_id_type=MESH,
        )

    def compose(whole, maps, k):
        high, low = split(maps[k, :WIDTH, :])
        joined = dot3(whole[k - 1], high, low)
        whole[k, :WIDTH] = joined[:WIDTH]
        whole[k, WIDTH:] = joined[WIDTH:] + maps[k, WIDTH:, :]

    to_slab = pltpu.make_async_remote_copy(
        src_ref=ywhole.at[3],
        dst_ref=gmaps.at[c * 4 + z],
        send_sem=gsend,
        recv_sem=grecv.at[c * 4 + z],
        device_id=slab_id,
        device_id_type=MESH,
    )

    @pl.when(yroot)
    def _():
        ymaps[y] = chain[SUBS, mine]
        for k in range(4):

            @pl.when(y != k)
            def _():
                arrival(ymaps, yrecv, k).wait_recv()

            if k == 0:
                ywhole[0] = ymaps[0]
            else:
                compose(ywhole, ymaps, k)

    @pl.when(yroot & jnp.logical_not(slab))
    def _():
        to_slab.start()

    onward = pltpu.make_async_remote_copy(
        src_ref=xout,
        dst_ref=xin,
        send_sem=xsem.at[0],
        recv_sem=xsem.at[1],
        device_id=device(jnp.minimum(x + 1, 3), c, z, y),
        device_id_type=MESH,
    )

    def to_yroot(k):
        return pltpu.make_async_remote_copy(
            src_ref=gout.at[k],
            dst_ref=gin,
            send_sem=esend.at[k],
            recv_sem=erecv,
            device_id=device(x, k // 4, k % 4, 2 * mine + k // 4),
            device_id_type=MESH,
        )

    @pl.when(slab)
    def _():
        gmaps[SLAB_Z] = ywhole[3]
        for k in range(8):
            if k != SLAB_Z:
                arrival(gmaps, grecv, k).wait_recv()
            if k == 0:
                gwhole[0] = gmaps[0]
            else:
                compose(gwhole, gmaps, k)

        @pl.when(x == 0)
        def _():
            xin[...] = jnp.broadcast_to(initial[pl.ds(mine, 1), :], (8, WIDTH))

        @pl.when(x > 0)
        def _():
            onward.wait_recv()

        columns = as_columns(xin[0:1, :])

        @pl.when(x < 3)
        def _():
            after = applied(columns, gwhole[7, :WIDTH, :], gwhole[7, WIDTH : WIDTH + 1, :])
            xout[...] = jnp.broadcast_to(after, (8, WIDTH))
            onward.start()

        for k in range(8):
            if k == 0:
                gout[0] = xin[...]
            else:
                entry = applied(
                    columns, gwhole[k - 1, :WIDTH, :], gwhole[k - 1, WIDTH : WIDTH + 1, :]
                )
                gout[k] = jnp.broadcast_to(entry, (8, WIDTH))
            if k != SLAB_Z:
                to_yroot(k).start()
            else:
                gin[...] = gout[k]

    def to_block(k):
        return pltpu.make_async_remote_copy(
            src_ref=fout.at[k],
            dst_ref=fin.at[mine],
            send_sem=fsend.at[k],
            recv_sem=frecv.at[mine],
            device_id=device(x, c, z, k),
            device_id_type=MESH,
        )

    @pl.when(yroot & jnp.logical_not(slab))
    def _():
        to_yroot(0).wait_recv()

    @pl.when(yroot)
    def _():
        columns = as_columns(gin[0:1, :])
        for k in range(4):
            if k == 0:
                fout[0] = gin[...]
            else:
                entry = applied(
                    columns, ywhole[k - 1, :WIDTH, :], ywhole[k - 1, WIDTH : WIDTH + 1, :]
                )
                fout[k] = jnp.broadcast_to(entry, (8, WIDTH))

            @pl.when(y != k)
            def _():
                to_block(k).start()

            @pl.when(y == k)
            def _():
                fin[mine] = fout[k]

    for s in range(2):

        @pl.when(root_at[s] != y)
        def _():
            pltpu.make_async_remote_copy(
                src_ref=fin.at[s],
                dst_ref=fin.at[s],
                send_sem=frecv.at[s],
                recv_sem=frecv.at[s],
                device_id=device(x, c, z, (y + 1) % 4),
                device_id_type=MESH,
            ).wait_recv()

    for s in range(2):
        row = fin[s, 0:1, :]
        columns = as_columns(row)
        state[s * SUBS : s * SUBS + 1, :] = row
        for sub in range(1, SUBS):
            at = s * SUBS + sub
            state[at : at + 1, :] = applied(
                columns, chain[sub, s, :WIDTH, :], chain[sub, s, WIDTH : WIDTH + 1, :]
            )
    now = state[...]
    for inner in range(SUB):
        turned = dot3(now, skew_hi[...], skew_lo[...])
        at = pl.ds(inner, 2 * SUBS, stride=SUB)
        steep = jnp.concatenate([slope2[half, at, :] for half in range(2)], axis=1)
        added = jnp.concatenate([offset2[half, at, :] for half in range(2)], axis=1)
        now = keep * now + steep * turned + added
        for half in range(2):
            out2[half, at, :] = now[:, half * 128 : half * 128 + 128]
    for half in range(2):
        out[:, half * 128 : half * 128 + 128] = out2[half]

    @pl.when(place < 127)
    def _():
        tail.wait_send()

    for s in range(2):

        @pl.when(root_at[s] != y)
        def _():
            to_root[s].wait_send()

    @pl.when(yroot & jnp.logical_not(slab))
    def _():
        to_slab.wait_send()

    @pl.when(slab & (x < 3))
    def _():
        onward.wait_send()

    @pl.when(slab)
    def _():
        for k in range(8):
            if k != SLAB_Z:
                to_yroot(k).wait_send()

    @pl.when(yroot)
    def _():
        for k in range(4):

            @pl.when(y != k)
            def _():
                to_block(k).wait_send()


def per_device(guess, inputs, initial, skew_base, in_weight, bias, rate):
    vmem = pl.BlockSpec(memory_space=pltpu.VMEM)
    dma = pltpu.SemaphoreType.DMA
    states = pl.pallas_call(
        kernel,
        out_shape=jax.ShapeDtypeStruct((2 * STEPS, WIDTH), F32),
        in_specs=[vmem] * 7,
        out_specs=vmem,
        scratch_shapes=[
            pltpu.VMEM((WIDTH, WIDTH), BF16),
            pltpu.VMEM((WIDTH, WIDTH), BF16),
            pltpu.VMEM((2, 8, WIDTH), F32),
            pltpu.VMEM((2, STEPS + 8, WIDTH), F32),
            pltpu.VMEM((2 * STEPS, WIDTH), F32),
            pltpu.VMEM((2 * STEPS, WIDTH), F32),
            pltpu.VMEM((SUBS + 1, 2, ROWS, WIDTH), F32),
            pltpu.VMEM((4, ROWS, WIDTH), F32),
            pltpu.VMEM((4, ROWS, WIDTH), F32),
            pltpu.VMEM((8, ROWS, WIDTH), F32),
            pltpu.VMEM((8, ROWS, WIDTH), F32),
            pltpu.VMEM((8, WIDTH), F32),
            pltpu.VMEM((8, WIDTH), F32),
            pltpu.VMEM((8, WIDTH), F32),
            pltpu.VMEM((8, 8, WIDTH), F32),
            pltpu.VMEM((2, 8, WIDTH), F32),
            pltpu.VMEM((4, 8, WIDTH), F32),
            pltpu.VMEM((8, WIDTH), F32),
            pltpu.VMEM((2, 2 * STEPS, 128), F32),
            pltpu.VMEM((2, 2 * STEPS, 128), F32),
            pltpu.VMEM((2, 2 * STEPS, 128), F32),
            dma((2,)),
            dma((2,)),
            dma((4,)),
            dma,
            dma((8,)),
            dma((2,)),
            dma((8,)),
            dma,
            dma((4,)),
            dma((2,)),
        ],
        compiler_params=pltpu.CompilerParams(
            collective_id=0, has_side_effects=True, vmem_limit_bytes=48 * 1024 * 1024
        ),
    )(
        guess,
        inputs,
        initial,
        skew_base,
        in_weight,
        bias.reshape(1, WIDTH),
        rate.reshape(1, WIDTH),
    )
    return states.reshape(2, STEPS, WIDTH)


def solution(mesh):
    return jax.shard_map(
        per_device,
        mesh=mesh,
        in_specs=(P(None, SEQ_GRP, None), P(None, SEQ_GRP, None), P(), P(), P(), P(), P()),
        out_specs=P(None, SEQ_GRP, None),
        check_vma=False,
    )
```

```python
import jax
import jax.numpy as jnp
from jax import lax
from jax.experimental import pallas as pl
from jax.experimental.pallas import tpu as pltpu
from jax.sharding import PartitionSpec as P

SEQ_GRP = ("seq", "grp")
MESH = pl.DeviceIdType.MESH
F32 = jnp.float32
BF16 = jnp.bfloat16
GAIN = 0.05

WIDTH = 256
STEPS = 32
SUB = 8
SUBS = STEPS // SUB
ROWS = WIDTH + 16
ZROOT = 1


def split(value):
    high = value.astype(BF16)
    return high, (value - high.astype(F32)).astype(BF16)


def dot(a, b):
    return jnp.dot(a, b, preferred_element_type=F32)


def dot3(value, high, low):
    top, rest = split(value)
    return dot(top, high) + dot(top, low) + dot(rest, high)


def compose(target, left, right):
    high, low = split(right[:WIDTH, :])
    joined = dot3(left[...], high, low)
    target[:WIDTH, :] = joined[:WIDTH]
    target[WIDTH:, :] = joined[WIDTH:] + right[WIDTH:, :]


def as_columns(row):
    turned = jnp.transpose(jnp.broadcast_to(row, (128, WIDTH)))
    return jnp.concatenate([turned, turned], axis=1)


def applied(columns, whole):
    moved = jnp.sum(whole[:WIDTH, :] * columns, axis=0, keepdims=True)
    return moved + whole[WIDTH : WIDTH + 1, :]


def tile(row):
    return jnp.broadcast_to(row, (8, WIDTH))


def kernel(
    guess_in, inputs_in, initial_in, base_in, weight_in, bias_in, rate_in, out,
    guess, inputs, initial, base, weight, bias, rate,
    skew, skew_hi, skew_lo, diag, before, prev, pre, slope, offset, slope2, offset2, out2,
    part, start, first, second, third, own,
    ymaps, ywhole, zmaps, zwhole, half, whole,
    xin, cin, ein, xout, cout, zout, zin, fout, fin, state,
    isem, psem, ysend, yrecv, zsend, zrecv, hsem, csem, xsend, xrecv, esend, erecv, fsend, frecv,
):
    seq_at, grp_at = lax.axis_index("seq"), lax.axis_index("grp")
    x, c = seq_at // 2, seq_at % 2
    z, y = grp_at // 4, grp_at % 4
    place = x * 32 + c * 16 + z * 4 + y

    def device(x, c, z, y):
        return (x * 2 + c, z * 4 + y)

    def block(index):
        return (index // 16, index % 16)

    mine = y // 2
    yroot = c == y % 2
    zroot = yroot & (z == ZROOT)
    below = yroot & (z != ZROOT)
    zroot0 = zroot & (c == 0)
    zroot1 = zroot & (c == 1)
    root_at = [2 * s + c for s in range(2)]

    def zroot_id(x, c):
        return device(x, c, ZROOT, 2 * mine + c)

    fetches = [
        pltpu.make_async_copy(source, target, isem.at[index])
        for index, (source, target) in enumerate(
            (
                (guess_in, guess),
                (inputs_in, inputs),
                (initial_in, initial),
                (base_in, base),
                (weight_in, weight),
                (bias_in, bias),
                (rate_in, rate),
            )
        )
    ]
    for index in (3, 6, 0, 1, 4, 5, 2):
        fetches[index].start()

    barrier = pltpu.get_barrier_semaphore()

    def greet(target):
        pl.semaphore_signal(barrier, inc=1, device_id=target, device_id_type=MESH)

    @pl.when(place > 0)
    def _():
        greet(block(place - 1))

    for s in range(2):

        @pl.when(root_at[s] != y)
        def _():
            greet(device(x, c, z, root_at[s]))

    @pl.when(yroot)
    def _():
        for k in range(1, 4):
            greet(device(x, c, z, (y + k) % 4))

    @pl.when(below)
    def _():
        greet(device(x, c, ZROOT, y))

    @pl.when(zroot)
    def _():
        for k in range(4):
            if k != ZROOT:
                greet(device(x, c, k, y))

    @pl.when(zroot1)
    def _():
        greet(zroot_id(x, 0))

    @pl.when(zroot & (x > 0))
    def _():
        greet(zroot_id(x - 1, 1))

    fetches[3].wait()
    skew_t = jnp.transpose(base[...]) - base[...]
    skew[...] = skew_t
    high, low = split(skew_t)
    skew_hi[...] = high
    skew_lo[...] = low
    fetches[6].wait()
    keep = 1.0 - rate[...]
    square = (WIDTH, WIDTH)
    eye = lax.broadcasted_iota(jnp.int32, square, 0) == lax.broadcasted_iota(jnp.int32, square, 1)
    diag[...] = jnp.where(eye, jnp.broadcast_to(keep, square), 0.0)
    top = (lax.broadcasted_iota(jnp.int32, (16, WIDTH), 0) == 0).astype(F32)

    fetches[0].wait()
    for s in range(2):
        prev[s, 0:8, :] = jnp.zeros((8, WIDTH), F32)
        prev[s, 8 : 8 + STEPS, :] = guess[s]
    for index in (1, 4, 5, 2):
        fetches[index].wait()
    pre[...] = dot(inputs[...].reshape(2 * STEPS, WIDTH), weight[...]) + bias[...]

    def slopes(earlier, before_tanh):
        lin = dot3(earlier, skew_hi[...], skew_lo[...])
        act = jnp.tanh(lin + before_tanh)
        steep = 1.0 - act * act
        return GAIN * steep, GAIN * (act - steep * lin)

    def keep_slopes(rows, steep, added):
        slope[rows, :] = steep
        offset[rows, :] = added
        for part_at in range(2):
            lanes = slice(part_at * 128, part_at * 128 + 128)
            slope2[part_at, rows, :] = steep[:, lanes]
            offset2[part_at, rows, :] = added[:, lanes]

    earlier = jnp.concatenate([prev[s, 7 : 7 + STEPS, :] for s in range(2)], axis=0)
    keep_slopes(slice(0, 2 * STEPS), *slopes(earlier, pre[...]))

    one, none = jnp.int32(1), jnp.int32(0)
    sends = jnp.where(place < 127, one, none) + jnp.where(yroot, 4 * one, 2 * one)
    sends = sends + jnp.where(below, one, none) + jnp.where(zroot, 3 * one, none)
    sends = sends + jnp.where(zroot0, one, none) + jnp.where(zroot1 & (x < 3), 2 * one, none)
    pl.semaphore_wait(barrier, sends)

    tail = pltpu.make_async_remote_copy(
        src_ref=guess.at[:, STEPS - 8 :, :],
        dst_ref=before,
        send_sem=psem.at[0],
        recv_sem=psem.at[1],
        device_id=block(jnp.minimum(place + 1, 127)),
        device_id_type=MESH,
    )

    @pl.when(place < 127)
    def _():
        tail.start()

    def of_step(target, at):
        target[:WIDTH, :] = diag[...] + skew[...] * slope[at : at + 1, :]
        target[WIDTH:, :] = top * offset[at : at + 1, :]

    def chains(s):
        for sub in range(SUBS):
            of_step(part.at[s, sub], s * STEPS + max(sub * SUB, 1))
        for inner in range(1, SUB):
            for sub in range(SUBS):
                at = max(sub * SUB, 1) + inner
                if at == SUB * (sub + 1):
                    continue
                at = at + s * STEPS
                held = part[s, sub]
                turned = dot3(held, skew_hi[...], skew_lo[...])
                moved = keep * held + slope[at : at + 1, :] * turned
                part[s, sub, :WIDTH, :] = moved[:WIDTH]
                part[s, sub, WIDTH:, :] = moved[WIDTH:] + top * offset[at : at + 1, :]

    def to_root(s):
        return pltpu.make_async_remote_copy(
            src_ref=own.at[s],
            dst_ref=ymaps.at[y],
            send_sem=ysend.at[s],
            recv_sem=yrecv.at[y],
            device_id=device(x, c, z, root_at[s]),
            device_id_type=MESH,
        )

    def landed(buffer, sem):
        return pltpu.make_async_remote_copy(
            src_ref=buffer,
            dst_ref=buffer,
            send_sem=sem,
            recv_sem=sem,
            device_id=device(x, c, z, (y + 1) % 4),
            device_id_type=MESH,
        )

    for s in range(2):
        chains(s)
        if s == 0:

            @pl.when(place > 0)
            def _():
                tail.wait_recv()
                for t in range(2):
                    prev[t, 7:8, :] = before[t, 7:8, :]

            @pl.when(place == 0)
            def _():
                for t in range(2):
                    prev[t, 7:8, :] = initial[t : t + 1, :]

            earlier = jnp.concatenate([prev[t, 7:15, :] for t in range(2)], axis=0)
            wanted = jnp.concatenate([pre[t * STEPS : t * STEPS + 8, :] for t in range(2)], axis=0)
            steep, added = slopes(earlier, wanted)
            for t in range(2):
                rows = slice(t * 8, t * 8 + 8)
                keep_slopes(slice(t * STEPS, t * STEPS + 8), steep[rows], added[rows])
        of_step(start, s * STEPS)
        compose(third, part.at[s, 2], part.at[s, 3])
        compose(first.at[s], start, part.at[s, 0])
        compose(second.at[s], first.at[s], part.at[s, 1])
        compose(own.at[s], second.at[s], third)

        @pl.when(root_at[s] != y)
        def _():
            to_root(s).start()

    to_zroot = pltpu.make_async_remote_copy(
        src_ref=ywhole.at[3],
        dst_ref=zmaps.at[z],
        send_sem=zsend,
        recv_sem=zrecv.at[z],
        device_id=device(x, c, ZROOT, y),
        device_id_type=MESH,
    )

    @pl.when(yroot)
    def _():
        ymaps[y] = own[mine]
        for k in range(4):

            @pl.when(y != k)
            def _():
                landed(ymaps.at[k], yrecv.at[k]).wait_recv()

            if k > 0:
                compose(ywhole.at[k], ymaps.at[0] if k == 1 else ywhole.at[k - 1], ymaps.at[k])

    @pl.when(below)
    def _():
        to_zroot.start()

    across = pltpu.make_async_remote_copy(
        src_ref=zwhole.at[3],
        dst_ref=half,
        send_sem=hsem.at[0],
        recv_sem=hsem.at[1],
        device_id=zroot_id(x, 1),
        device_id_type=MESH,
    )
    across0 = pltpu.make_async_remote_copy(
        src_ref=cout,
        dst_ref=cin,
        send_sem=csem.at[0],
        recv_sem=csem.at[1],
        device_id=zroot_id(x, 1),
        device_id_type=MESH,
    )

    def onward(core):
        return pltpu.make_async_remote_copy(
            src_ref=xout,
            dst_ref=xin,
            send_sem=xsend.at[core],
            recv_sem=xrecv,
            device_id=zroot_id(jnp.minimum(x + 1, 3), core),
            device_id_type=MESH,
        )

    def to_yroot(k):
        return pltpu.make_async_remote_copy(
            src_ref=zout.at[k],
            dst_ref=zin,
            send_sem=esend.at[k],
            recv_sem=erecv,
            device_id=device(x, c, k, y),
            device_id_type=MESH,
        )

    def zprefix(k):
        return zmaps.at[0] if k == 0 else zwhole.at[k]

    @pl.when(zroot)
    def _():
        for k in range(4):
            if k != ZROOT:
                landed(zmaps.at[k], zrecv.at[k]).wait_recv()
            if k > 0:
                compose(zwhole.at[k], zprefix(k - 1), ywhole.at[3] if k == ZROOT else zmaps.at[k])

        @pl.when((c == 0) & (x == 0))
        def _():
            given = initial[pl.ds(mine, 1), :]
            ein[...] = tile(given)
            cout[...] = tile(applied(as_columns(given), zwhole.at[3]))
            across0.start()

        @pl.when((c == 0) & (x > 0))
        def _():
            across.start()
            landed(xin, xrecv).wait_recv()
            ein[...] = xin[...]

        @pl.when((c == 1) & (x == 0))
        def _():
            across0.wait_recv()
            ein[...] = cin[...]
            xout[...] = tile(applied(as_columns(cin[0:1, :]), zwhole.at[3]))
            for core in (1, 0):
                onward(core).start()

        @pl.when((c == 1) & (x > 0))
        def _():
            across.wait_recv()
            compose(whole, half, zwhole.at[3])
            landed(xin, xrecv).wait_recv()
            columns = as_columns(xin[0:1, :])

            @pl.when(x < 3)
            def _():
                xout[...] = tile(applied(columns, whole))
                for core in (1, 0):
                    onward(core).start()

            ein[...] = tile(applied(columns, half))

        columns = as_columns(ein[0:1, :])
        for k in range(4):
            zout[k] = ein[...] if k == 0 else tile(applied(columns, zprefix(k - 1)))
            if k == ZROOT:
                zin[...] = zout[k]
            else:
                to_yroot(k).start()

    def to_block(k):
        return pltpu.make_async_remote_copy(
            src_ref=fout.at[k],
            dst_ref=fin.at[mine],
            send_sem=fsend.at[k],
            recv_sem=frecv.at[mine],
            device_id=device(x, c, z, k),
            device_id_type=MESH,
        )

    @pl.when(below)
    def _():
        landed(zin, erecv).wait_recv()

    @pl.when(yroot)
    def _():
        columns = as_columns(zin[0:1, :])
        for k in range(4):
            if k == 0:
                fout[0] = zin[...]
            else:
                fout[k] = tile(applied(columns, ymaps.at[0] if k == 1 else ywhole.at[k - 1]))

            @pl.when(y != k)
            def _():
                to_block(k).start()

            @pl.when(y == k)
            def _():
                fin[mine] = fout[k]

    for s in range(2):

        @pl.when(root_at[s] != y)
        def _():
            landed(fin.at[s], frecv.at[s]).wait_recv()

    for s in range(2):
        entry = fin[s, 0:1, :]
        columns = as_columns(entry)
        middle = applied(columns, second.at[s])
        at = s * SUBS
        state[at : at + 1, :] = entry
        state[at + 1 : at + 2, :] = applied(columns, first.at[s])
        state[at + 2 : at + 3, :] = middle
        state[at + 3 : at + 4, :] = applied(as_columns(middle), part.at[s, 2])
    now = state[...]
    for inner in range(SUB):
        turned = dot3(now, skew_hi[...], skew_lo[...])
        at = pl.ds(inner, 2 * SUBS, stride=SUB)
        steep = jnp.concatenate([slope2[lanes, at, :] for lanes in range(2)], axis=1)
        added = jnp.concatenate([offset2[lanes, at, :] for lanes in range(2)], axis=1)
        now = keep * now + steep * turned + added
        for lanes in range(2):
            out2[lanes, at, :] = now[:, lanes * 128 : lanes * 128 + 128]
    for lanes in range(2):
        out[:, lanes * 128 : lanes * 128 + 128] = out2[lanes]

    @pl.when(place < 127)
    def _():
        tail.wait_send()

    for s in range(2):

        @pl.when(root_at[s] != y)
        def _():
            to_root(s).wait_send()

    @pl.when(below)
    def _():
        to_zroot.wait_send()

    @pl.when(zroot0 & (x == 0))
    def _():
        across0.wait_send()

    @pl.when(zroot0 & (x > 0))
    def _():
        across.wait_send()

    @pl.when(zroot1 & (x < 3))
    def _():
        for core in (1, 0):
            onward(core).wait_send()

    @pl.when(zroot)
    def _():
        for k in range(4):
            if k != ZROOT:
                to_yroot(k).wait_send()

    @pl.when(yroot)
    def _():
        for k in range(4):

            @pl.when(y != k)
            def _():
                to_block(k).wait_send()


def per_device(guess, inputs, initial, skew_base, in_weight, bias, rate):
    dma = pltpu.SemaphoreType.DMA

    def f32(*shape):
        return pltpu.VMEM(shape, F32)

    maps = (ROWS, WIDTH)
    states = pl.pallas_call(
        kernel,
        out_shape=jax.ShapeDtypeStruct((2 * STEPS, WIDTH), F32),
        in_specs=[pl.BlockSpec(memory_space=pl.ANY)] * 7,
        out_specs=pl.BlockSpec(memory_space=pltpu.VMEM),
        scratch_shapes=[
            f32(2, STEPS, WIDTH),
            pltpu.VMEM((2, STEPS, WIDTH), BF16),
            f32(2, WIDTH),
            f32(WIDTH, WIDTH),
            pltpu.VMEM((WIDTH, WIDTH), BF16),
            f32(1, WIDTH),
            f32(1, WIDTH),
            f32(WIDTH, WIDTH),
            pltpu.VMEM((WIDTH, WIDTH), BF16),
            pltpu.VMEM((WIDTH, WIDTH), BF16),
            f32(WIDTH, WIDTH),
            f32(2, 8, WIDTH),
            f32(2, STEPS + 8, WIDTH),
            f32(2 * STEPS, WIDTH),
            f32(2 * STEPS, WIDTH),
            f32(2 * STEPS, WIDTH),
            f32(2, 2 * STEPS, 128),
            f32(2, 2 * STEPS, 128),
            f32(2, 2 * STEPS, 128),
            f32(2, SUBS, *maps),
            f32(*maps),
            f32(2, *maps),
            f32(2, *maps),
            f32(*maps),
            f32(2, *maps),
            f32(4, *maps),
            f32(4, *maps),
            f32(4, *maps),
            f32(4, *maps),
            f32(*maps),
            f32(*maps),
            f32(8, WIDTH),
            f32(8, WIDTH),
            f32(8, WIDTH),
            f32(8, WIDTH),
            f32(8, WIDTH),
            f32(4, 8, WIDTH),
            f32(8, WIDTH),
            f32(4, 8, WIDTH),
            f32(2, 8, WIDTH),
            f32(8, WIDTH),
            dma((7,)),
            dma((2,)),
            dma((2,)),
            dma((4,)),
            dma,
            dma((4,)),
            dma((2,)),
            dma((2,)),
            dma((2,)),
            dma,
            dma((4,)),
            dma,
            dma((4,)),
            dma((2,)),
        ],
        compiler_params=pltpu.CompilerParams(
            collective_id=0, has_side_effects=True, vmem_limit_bytes=60 * 1024 * 1024
        ),
    )(
        guess,
        inputs,
        initial,
        skew_base,
        in_weight,
        bias.reshape(1, WIDTH),
        rate.reshape(1, WIDTH),
    )
    return states.reshape(2, STEPS, WIDTH)


def solution(mesh):
    return jax.shard_map(
        per_device,
        mesh=mesh,
        in_specs=(P(None, SEQ_GRP, None), P(None, SEQ_GRP, None), P(), P(), P(), P(), P()),
        out_specs=P(None, SEQ_GRP, None),
        check_vma=False,
    )
```

```python
import jax
import jax.numpy as jnp
from jax import lax
from jax.experimental import pallas as pl
from jax.experimental.pallas import tpu as pltpu
from jax.sharding import PartitionSpec as P

SEQ_GRP = ("seq", "grp")
MESH = pl.DeviceIdType.MESH
F32 = jnp.float32
BF16 = jnp.bfloat16
GAIN = 0.05

WIDTH = 256
STEPS = 32
SUB = 8
SUBS = STEPS // SUB
ROWS = WIDTH + 16
ZROOT = 1


def split(value):
    high = value.astype(BF16)
    return high, (value - high.astype(F32)).astype(BF16)


def dot(a, b):
    return jnp.dot(a, b, preferred_element_type=F32)


def dot3(value, high, low):
    top, rest = split(value)
    return dot(top, high) + dot(top, low) + dot(rest, high)


def compose(target, left, right):
    high, low = split(right[:WIDTH, :])
    joined = dot3(left[...], high, low)
    target[:WIDTH, :] = joined[:WIDTH]
    target[WIDTH:, :] = joined[WIDTH:] + right[WIDTH:, :]


def as_columns(row):
    turned = jnp.transpose(jnp.broadcast_to(row, (128, WIDTH)))
    return jnp.concatenate([turned, turned], axis=1)


def applied(columns, whole):
    moved = jnp.sum(whole[:WIDTH, :] * columns, axis=0, keepdims=True)
    return moved + whole[WIDTH : WIDTH + 1, :]


def tile(row):
    return jnp.broadcast_to(row, (8, WIDTH))


def kernel(
    guess_in, inputs_in, initial_in, base_in, weight_in, bias_in, rate_in, out,
    guess, inputs, initial, base, weight, bias, rate,
    skew, skew_hi, skew_lo, diag, before, prev, pre, slope, offset, slope2, offset2, out2,
    part, start, first, second, third, own,
    ymaps, ywhole, zmaps, zwhole, half, whole,
    pmaps, xin, cin, ein, xout, cout, zout, fin, entries, state,
    isem, psem, ysend, yrecv, zsend, zrecv, hsem, csem, xsend, xrecv, esend, erecv, fsend, frecv,
):
    seq_at, grp_at = lax.axis_index("seq"), lax.axis_index("grp")
    x, c = seq_at // 2, seq_at % 2
    z, y = grp_at // 4, grp_at % 4
    place = x * 32 + c * 16 + z * 4 + y

    def device(x, c, z, y):
        return (x * 2 + c, z * 4 + y)

    def block(index):
        return (index // 16, index % 16)

    mine = y // 2
    yroot = c == y % 2
    zroot = yroot & (z == ZROOT)
    below = yroot & (z != ZROOT)
    zroot0 = zroot & (c == 0)
    zroot1 = zroot & (c == 1)
    root_at = [2 * s + c for s in range(2)]

    def zroot_id(x, c):
        return device(x, c, ZROOT, 2 * mine + c)

    fetches = [
        pltpu.make_async_copy(source, target, isem.at[index])
        for index, (source, target) in enumerate(
            (
                (guess_in, guess),
                (inputs_in, inputs),
                (initial_in, initial),
                (base_in, base),
                (weight_in, weight),
                (bias_in, bias),
                (rate_in, rate),
            )
        )
    ]
    for index in (3, 6, 0, 1, 4, 5, 2):
        fetches[index].start()

    barrier = pltpu.get_barrier_semaphore()

    def greet(target):
        pl.semaphore_signal(barrier, inc=1, device_id=target, device_id_type=MESH)

    @pl.when(place > 0)
    def _():
        greet(block(place - 1))

    for s in range(2):

        @pl.when(root_at[s] != y)
        def _():
            greet(device(x, c, z, root_at[s]))

    @pl.when(yroot)
    def _():
        for k in range(1, 4):
            greet(device(x, c, z, (y + k) % 4))

    @pl.when(zroot)
    def _():
        for k in range(4):
            if k != ZROOT:
                greet(device(x, c, k, y))

    for s in range(2):

        @pl.when(jnp.logical_not(zroot & (mine == s)))
        def _():
            greet(device(x, c, ZROOT, root_at[s]))

    @pl.when(zroot1)
    def _():
        greet(zroot_id(x, 0))

    @pl.when(zroot & (x > 0))
    def _():
        greet(zroot_id(x - 1, 1))

    fetches[3].wait()
    skew_t = jnp.transpose(base[...]) - base[...]
    skew[...] = skew_t
    high, low = split(skew_t)
    skew_hi[...] = high
    skew_lo[...] = low
    fetches[6].wait()
    keep = 1.0 - rate[...]
    square = (WIDTH, WIDTH)
    eye = lax.broadcasted_iota(jnp.int32, square, 0) == lax.broadcasted_iota(jnp.int32, square, 1)
    diag[...] = jnp.where(eye, jnp.broadcast_to(keep, square), 0.0)
    top = (lax.broadcasted_iota(jnp.int32, (16, WIDTH), 0) == 0).astype(F32)

    fetches[0].wait()
    for s in range(2):
        prev[s, 0:8, :] = jnp.zeros((8, WIDTH), F32)
        prev[s, 8 : 8 + STEPS, :] = guess[s]
    for index in (1, 4, 5, 2):
        fetches[index].wait()
    pre[...] = dot(inputs[...].reshape(2 * STEPS, WIDTH), weight[...]) + bias[...]

    def slopes(earlier, before_tanh):
        lin = dot3(earlier, skew_hi[...], skew_lo[...])
        act = jnp.tanh(lin + before_tanh)
        steep = 1.0 - act * act
        return GAIN * steep, GAIN * (act - steep * lin)

    def keep_slopes(rows, steep, added):
        slope[rows, :] = steep
        offset[rows, :] = added
        for part_at in range(2):
            lanes = slice(part_at * 128, part_at * 128 + 128)
            slope2[part_at, rows, :] = steep[:, lanes]
            offset2[part_at, rows, :] = added[:, lanes]

    earlier = jnp.concatenate([prev[s, 7 : 7 + STEPS, :] for s in range(2)], axis=0)
    keep_slopes(slice(0, 2 * STEPS), *slopes(earlier, pre[...]))

    def of_step(target, at):
        target[:WIDTH, :] = diag[...] + skew[...] * slope[at : at + 1, :]
        target[WIDTH:, :] = top * offset[at : at + 1, :]

    def chains(s, begin, end):
        for inner in range(begin, end):
            if inner == 0:
                for sub in range(SUBS):
                    of_step(part.at[s, sub], s * STEPS + max(sub * SUB, 1))
                continue
            for sub in range(SUBS):
                at = max(sub * SUB, 1) + inner
                if at == SUB * (sub + 1):
                    continue
                at = at + s * STEPS
                held = part[s, sub]
                turned = dot3(held, skew_hi[...], skew_lo[...])
                moved = keep * held + slope[at : at + 1, :] * turned
                part[s, sub, :WIDTH, :] = moved[:WIDTH]
                part[s, sub, WIDTH:, :] = moved[WIDTH:] + top * offset[at : at + 1, :]

    tail = pltpu.make_async_remote_copy(
        src_ref=guess.at[:, STEPS - 8 :, :],
        dst_ref=before,
        send_sem=psem.at[0],
        recv_sem=psem.at[1],
        device_id=block(jnp.minimum(place + 1, 127)),
        device_id_type=MESH,
    )

    def to_root(s):
        return pltpu.make_async_remote_copy(
            src_ref=own.at[s],
            dst_ref=ymaps.at[y],
            send_sem=ysend.at[s],
            recv_sem=yrecv.at[y],
            device_id=device(x, c, z, root_at[s]),
            device_id_type=MESH,
        )

    def landed(buffer, sem):
        return pltpu.make_async_remote_copy(
            src_ref=buffer,
            dst_ref=buffer,
            send_sem=sem,
            recv_sem=sem,
            device_id=device(x, c, z, (y + 1) % 4),
            device_id_type=MESH,
        )

    chains(0, 0, SUB)

    one, none = jnp.int32(1), jnp.int32(0)
    sends = jnp.where(place < 127, one, none) + jnp.where(yroot, 4 * one, 2 * one)
    sends = sends + jnp.where(below, one, none) + jnp.where(zroot, 15 * one, none)
    sends = sends + jnp.where(zroot0, one, none) + jnp.where(zroot1 & (x < 3), 2 * one, none)
    pl.semaphore_wait(barrier, sends)


    @pl.when(place < 127)
    def _():
        tail.start()

    chains(1, 0, SUB // 2)

    @pl.when(place > 0)
    def _():
        tail.wait_recv()
        for t in range(2):
            prev[t, 7:8, :] = before[t, 7:8, :]

    @pl.when(place == 0)
    def _():
        for t in range(2):
            prev[t, 7:8, :] = initial[t : t + 1, :]

    earlier = jnp.concatenate([prev[t, 7:15, :] for t in range(2)], axis=0)
    wanted = jnp.concatenate([pre[t * STEPS : t * STEPS + 8, :] for t in range(2)], axis=0)
    steep, added = slopes(earlier, wanted)
    for t in range(2):
        rows = slice(t * 8, t * 8 + 8)
        keep_slopes(slice(t * STEPS, t * STEPS + 8), steep[rows], added[rows])

    for s in range(2):
        if s == 1:
            chains(1, SUB // 2, SUB)
        of_step(start, s * STEPS)
        compose(third, part.at[s, 2], part.at[s, 3])
        compose(first.at[s], start, part.at[s, 0])
        compose(second.at[s], first.at[s], part.at[s, 1])
        compose(own.at[s], second.at[s], third)

        @pl.when(root_at[s] != y)
        def _():
            to_root(s).start()

    to_zroot = pltpu.make_async_remote_copy(
        src_ref=ywhole.at[3],
        dst_ref=zmaps.at[z],
        send_sem=zsend,
        recv_sem=zrecv.at[z],
        device_id=device(x, c, ZROOT, y),
        device_id_type=MESH,
    )

    @pl.when(yroot)
    def _():
        ymaps[y] = own[mine]
        for k in range(4):

            @pl.when(y != k)
            def _():
                landed(ymaps.at[k], yrecv.at[k]).wait_recv()

            if k > 0:
                compose(ywhole.at[k], ymaps.at[0] if k == 1 else ywhole.at[k - 1], ymaps.at[k])

    @pl.when(below)
    def _():
        to_zroot.start()

    def prefix_out(k):
        return pltpu.make_async_remote_copy(
            src_ref=ymaps.at[0] if k == 1 else ywhole.at[k - 1],
            dst_ref=pmaps.at[mine],
            send_sem=fsend.at[k],
            recv_sem=frecv.at[mine],
            device_id=device(x, c, z, k),
            device_id_type=MESH,
        )

    @pl.when(yroot)
    def _():
        for k in range(1, 4):

            @pl.when(y != k)
            def _():
                prefix_out(k).start()

    across = pltpu.make_async_remote_copy(
        src_ref=zwhole.at[3],
        dst_ref=half,
        send_sem=hsem.at[0],
        recv_sem=hsem.at[1],
        device_id=zroot_id(x, 1),
        device_id_type=MESH,
    )
    across0 = pltpu.make_async_remote_copy(
        src_ref=cout,
        dst_ref=cin,
        send_sem=csem.at[0],
        recv_sem=csem.at[1],
        device_id=zroot_id(x, 1),
        device_id_type=MESH,
    )

    def onward(core):
        return pltpu.make_async_remote_copy(
            src_ref=xout,
            dst_ref=xin,
            send_sem=xsend.at[core],
            recv_sem=xrecv,
            device_id=zroot_id(jnp.minimum(x + 1, 3), core),
            device_id_type=MESH,
        )

    def entry_out(k, at):
        return pltpu.make_async_remote_copy(
            src_ref=zout.at[k],
            dst_ref=fin.at[mine],
            send_sem=esend.at[k * 4 + at],
            recv_sem=erecv.at[mine],
            device_id=device(x, c, k, at),
            device_id_type=MESH,
        )

    def zprefix(k):
        return zmaps.at[0] if k == 0 else zwhole.at[k]

    @pl.when(zroot)
    def _():
        for k in range(4):
            if k != ZROOT:
                landed(zmaps.at[k], zrecv.at[k]).wait_recv()
            if k > 0:
                compose(zwhole.at[k], zprefix(k - 1), ywhole.at[3] if k == ZROOT else zmaps.at[k])

        @pl.when((c == 0) & (x == 0))
        def _():
            given = initial[pl.ds(mine, 1), :]
            ein[...] = tile(given)
            cout[...] = tile(applied(as_columns(given), zwhole.at[3]))
            across0.start()

        @pl.when((c == 0) & (x > 0))
        def _():
            across.start()
            landed(xin, xrecv).wait_recv()
            ein[...] = xin[...]

        @pl.when((c == 1) & (x == 0))
        def _():
            across0.wait_recv()
            ein[...] = cin[...]
            xout[...] = tile(applied(as_columns(cin[0:1, :]), zwhole.at[3]))
            for core in (1, 0):
                onward(core).start()

        @pl.when((c == 1) & (x > 0))
        def _():
            across.wait_recv()
            compose(whole, half, zwhole.at[3])
            landed(xin, xrecv).wait_recv()
            columns = as_columns(xin[0:1, :])

            @pl.when(x < 3)
            def _():
                xout[...] = tile(applied(columns, whole))
                for core in (1, 0):
                    onward(core).start()

            ein[...] = tile(applied(columns, half))

        columns = as_columns(ein[0:1, :])
        for k in range(4):
            zout[k] = ein[...] if k == 0 else tile(applied(columns, zprefix(k - 1)))
            for at in range(4):
                if k != ZROOT:
                    entry_out(k, at).start()
                else:

                    @pl.when(y != at)
                    def _():
                        entry_out(k, at).start()

        fin[mine] = zout[ZROOT]

    for s in range(2):

        @pl.when((y > 0) & (root_at[s] != y))
        def _():
            landed(pmaps.at[s], frecv.at[s]).wait_recv()

    @pl.when(yroot & (y == 1))
    def _():
        pmaps[mine] = ymaps[0]

    for k in range(2, 4):

        @pl.when(yroot & (y == k))
        def _():
            pmaps[mine] = ywhole[k - 1]

    for s in range(2):

        @pl.when(jnp.logical_not(zroot & (mine == s)))
        def _():
            landed(fin.at[s], erecv.at[s]).wait_recv()

        given = fin[s, 0:1, :]
        entries[s] = fin[s]

        @pl.when(y > 0)
        def _():
            entries[s] = tile(applied(as_columns(given), pmaps.at[s]))

    for s in range(2):
        entry = entries[s, 0:1, :]
        columns = as_columns(entry)
        middle = applied(columns, second.at[s])
        at = s * SUBS
        state[at : at + 1, :] = entry
        state[at + 1 : at + 2, :] = applied(columns, first.at[s])
        state[at + 2 : at + 3, :] = middle
        state[at + 3 : at + 4, :] = applied(as_columns(middle), part.at[s, 2])
    now = state[...]
    for inner in range(SUB):
        turned = dot3(now, skew_hi[...], skew_lo[...])
        at = pl.ds(inner, 2 * SUBS, stride=SUB)
        steep = jnp.concatenate([slope2[lanes, at, :] for lanes in range(2)], axis=1)
        added = jnp.concatenate([offset2[lanes, at, :] for lanes in range(2)], axis=1)
        now = keep * now + steep * turned + added
        for lanes in range(2):
            out2[lanes, at, :] = now[:, lanes * 128 : lanes * 128 + 128]
    for lanes in range(2):
        out[:, lanes * 128 : lanes * 128 + 128] = out2[lanes]

    @pl.when(place < 127)
    def _():
        tail.wait_send()

    for s in range(2):

        @pl.when(root_at[s] != y)
        def _():
            to_root(s).wait_send()

    @pl.when(below)
    def _():
        to_zroot.wait_send()

    @pl.when(zroot0 & (x == 0))
    def _():
        across0.wait_send()

    @pl.when(zroot0 & (x > 0))
    def _():
        across.wait_send()

    @pl.when(zroot1 & (x < 3))
    def _():
        for core in (1, 0):
            onward(core).wait_send()

    @pl.when(zroot)
    def _():
        for k in range(4):
            for at in range(4):
                if k != ZROOT:
                    entry_out(k, at).wait_send()
                else:

                    @pl.when(y != at)
                    def _():
                        entry_out(k, at).wait_send()

    @pl.when(yroot)
    def _():
        for k in range(1, 4):

            @pl.when(y != k)
            def _():
                prefix_out(k).wait_send()


def per_device(guess, inputs, initial, skew_base, in_weight, bias, rate):
    dma = pltpu.SemaphoreType.DMA

    def f32(*shape):
        return pltpu.VMEM(shape, F32)

    maps = (ROWS, WIDTH)
    states = pl.pallas_call(
        kernel,
        out_shape=jax.ShapeDtypeStruct((2 * STEPS, WIDTH), F32),
        in_specs=[pl.BlockSpec(memory_space=pltpu.HBM)] * 7,
        out_specs=pl.BlockSpec(memory_space=pltpu.VMEM),
        scratch_shapes=[
            f32(2, STEPS, WIDTH),
            pltpu.VMEM((2, STEPS, WIDTH), BF16),
            f32(2, WIDTH),
            f32(WIDTH, WIDTH),
            pltpu.VMEM((WIDTH, WIDTH), BF16),
            f32(1, WIDTH),
            f32(1, WIDTH),
            f32(WIDTH, WIDTH),
            pltpu.VMEM((WIDTH, WIDTH), BF16),
            pltpu.VMEM((WIDTH, WIDTH), BF16),
            f32(WIDTH, WIDTH),
            f32(2, 8, WIDTH),
            f32(2, STEPS + 8, WIDTH),
            f32(2 * STEPS, WIDTH),
            f32(2 * STEPS, WIDTH),
            f32(2 * STEPS, WIDTH),
            f32(2, 2 * STEPS, 128),
            f32(2, 2 * STEPS, 128),
            f32(2, 2 * STEPS, 128),
            f32(2, SUBS, *maps),
            f32(*maps),
            f32(2, *maps),
            f32(2, *maps),
            f32(*maps),
            f32(2, *maps),
            f32(4, *maps),
            f32(4, *maps),
            f32(4, *maps),
            f32(4, *maps),
            f32(*maps),
            f32(*maps),
            f32(2, *maps),
            f32(8, WIDTH),
            f32(8, WIDTH),
            f32(8, WIDTH),
            f32(8, WIDTH),
            f32(8, WIDTH),
            f32(4, 8, WIDTH),
            f32(2, 8, WIDTH),
            f32(2, 8, WIDTH),
            f32(8, WIDTH),
            dma((7,)),
            dma((2,)),
            dma((2,)),
            dma((4,)),
            dma,
            dma((4,)),
            dma((2,)),
            dma((2,)),
            dma((2,)),
            dma,
            dma((16,)),
            dma((2,)),
            dma((4,)),
            dma((2,)),
        ],
        compiler_params=pltpu.CompilerParams(
            collective_id=0, has_side_effects=True, vmem_limit_bytes=60 * 1024 * 1024
        ),
    )(
        guess,
        inputs,
        initial,
        skew_base,
        in_weight,
        bias.reshape(1, WIDTH),
        rate.reshape(1, WIDTH),
    )
    return states.reshape(2, STEPS, WIDTH)


def solution(mesh):
    return jax.shard_map(
        per_device,
        mesh=mesh,
        in_specs=(P(None, SEQ_GRP, None), P(None, SEQ_GRP, None), P(), P(), P(), P(), P()),
        out_specs=P(None, SEQ_GRP, None),
        check_vma=False,
    )
```

```python
import jax
import jax.numpy as jnp
from jax import lax
from jax.experimental import pallas as pl
from jax.experimental.pallas import tpu as pltpu
from jax.sharding import PartitionSpec as P

SEQ_GRP = ("seq", "grp")
MESH = pl.DeviceIdType.MESH
F32 = jnp.float32
BF16 = jnp.bfloat16
GAIN = 0.05

WIDTH = 256
STEPS = 32
SUB = 8
SUBS = STEPS // SUB
ROWS = WIDTH + 16
ZROOT = 1
HALF = ROWS // 2


def split(value):
    high = value.astype(BF16)
    return high, (value - high.astype(F32)).astype(BF16)


def dot(a, b):
    return jnp.dot(a, b, preferred_element_type=F32)


def dot3(value, high, low):
    top, rest = split(value)
    return dot(top, high) + dot(top, low) + dot(rest, high)


def compose(target, left, right):
    high, low = split(right[:WIDTH, :])
    joined = dot3(left[...], high, low)
    target[:WIDTH, :] = joined[:WIDTH]
    target[WIDTH:, :] = joined[WIDTH:] + right[WIDTH:, :]


def as_columns(row):
    turned = jnp.transpose(jnp.broadcast_to(row, (128, WIDTH)))
    return jnp.concatenate([turned, turned], axis=1)


def applied(columns, whole):
    moved = jnp.sum(whole[:WIDTH, :] * columns, axis=0, keepdims=True)
    return moved + whole[WIDTH : WIDTH + 1, :]


def tile(row):
    return jnp.broadcast_to(row, (8, WIDTH))


def kernel(
    guess_in, inputs_in, initial_in, base_in, weight_in, bias_in, rate_in, out,
    guess, inputs, initial, base, weight, bias, rate,
    skew, skew_hi, skew_lo, diag, before, prev, pre, slope, offset, slope2, offset2, out2,
    part, start, first, second, third, own,
    ymaps, ywhole, zmaps, zwhole, half, whole,
    pmaps, xin, cin, ein, xout, cout, zout, fin, entries, state, yheld, zheld,
    isem, psem, ysend, yrecv, yrelay, zsend, zrecv, zrelay, hsem, csem, xsend, xrecv, esend, erecv, fsend, frecv,
):
    seq_at, grp_at = lax.axis_index("seq"), lax.axis_index("grp")
    x, c = seq_at // 2, seq_at % 2
    z, y = grp_at // 4, grp_at % 4
    place = x * 32 + c * 16 + z * 4 + y

    def device(x, c, z, y):
        return (x * 2 + c, z * 4 + y)

    def block(index):
        return (index // 16, index % 16)

    mine = 1 - y // 2
    yroot = c == y % 2
    zroot = yroot & (z == ZROOT)
    below = yroot & (z != ZROOT)
    first_z, last_z = yroot & (z == 0), yroot & (z == 3)
    zroot0 = zroot & (c == 0)
    zroot1 = zroot & (c == 1)
    root_at = [2 * (1 - s) + c for s in range(2)]

    def zroot_id(x, c):
        return device(x, c, ZROOT, 2 * (1 - mine) + c)

    fetches = [
        pltpu.make_async_copy(source, target, isem.at[index])
        for index, (source, target) in enumerate(
            (
                (guess_in, guess),
                (inputs_in, inputs),
                (initial_in, initial),
                (base_in, base),
                (weight_in, weight),
                (bias_in, bias),
                (rate_in, rate),
            )
        )
    ]
    for index in (3, 6, 0, 1, 4, 5, 2):
        fetches[index].start()

    barrier = pltpu.get_barrier_semaphore()

    def greet(target):
        pl.semaphore_signal(barrier, inc=1, device_id=target, device_id_type=MESH)

    @pl.when(place > 0)
    def _():
        greet(block(place - 1))

    for s in range(2):

        @pl.when(root_at[s] != y)
        def _():
            greet(device(x, c, z, root_at[s]))

    @pl.when(yroot)
    def _():
        for k in range(1, 4):
            greet(device(x, c, z, (y + k) % 4))

    @pl.when(zroot)
    def _():
        for k in range(4):
            if k != ZROOT:
                greet(device(x, c, k, y))

    @pl.when(first_z)
    def _():
        greet(device(x, c, 3, y))

    for s in range(2):

        @pl.when(jnp.logical_not(zroot & (mine == s)))
        def _():
            greet(device(x, c, ZROOT, root_at[s]))

    @pl.when(zroot1)
    def _():
        greet(zroot_id(x, 0))

    @pl.when(zroot & (x > 0))
    def _():
        greet(zroot_id(x - 1, 1))

    fetches[3].wait()
    skew_t = jnp.transpose(base[...]) - base[...]
    skew[...] = skew_t
    high, low = split(skew_t)
    skew_hi[...] = high
    skew_lo[...] = low
    fetches[6].wait()
    keep = 1.0 - rate[...]
    square = (WIDTH, WIDTH)
    eye = lax.broadcasted_iota(jnp.int32, square, 0) == lax.broadcasted_iota(jnp.int32, square, 1)
    diag[...] = jnp.where(eye, jnp.broadcast_to(keep, square), 0.0)
    top = (lax.broadcasted_iota(jnp.int32, (16, WIDTH), 0) == 0).astype(F32)

    fetches[0].wait()
    for s in range(2):
        prev[s, 0:8, :] = jnp.zeros((8, WIDTH), F32)
        prev[s, 8 : 8 + STEPS, :] = guess[s]
    for index in (1, 4, 5, 2):
        fetches[index].wait()
    pre[...] = dot(inputs[...].reshape(2 * STEPS, WIDTH), weight[...]) + bias[...]

    def slopes(earlier, before_tanh):
        lin = dot3(earlier, skew_hi[...], skew_lo[...])
        act = jnp.tanh(lin + before_tanh)
        steep = 1.0 - act * act
        return GAIN * steep, GAIN * (act - steep * lin)

    def keep_slopes(rows, steep, added):
        slope[rows, :] = steep
        offset[rows, :] = added
        for part_at in range(2):
            lanes = slice(part_at * 128, part_at * 128 + 128)
            slope2[part_at, rows, :] = steep[:, lanes]
            offset2[part_at, rows, :] = added[:, lanes]

    earlier = jnp.concatenate([prev[s, 7 : 7 + STEPS, :] for s in range(2)], axis=0)
    keep_slopes(slice(0, 2 * STEPS), *slopes(earlier, pre[...]))

    def of_step(target, at):
        target[:WIDTH, :] = diag[...] + skew[...] * slope[at : at + 1, :]
        target[WIDTH:, :] = top * offset[at : at + 1, :]

    def chains(s, begin, end):
        for inner in range(begin, end):
            if inner == 0:
                for sub in range(SUBS):
                    of_step(part.at[s, sub], s * STEPS + max(sub * SUB, 1))
                continue
            for sub in range(SUBS):
                at = max(sub * SUB, 1) + inner
                if at == SUB * (sub + 1):
                    continue
                at = at + s * STEPS
                held = part[s, sub]
                turned = dot3(held, skew_hi[...], skew_lo[...])
                moved = keep * held + slope[at : at + 1, :] * turned
                part[s, sub, :WIDTH, :] = moved[:WIDTH]
                part[s, sub, WIDTH:, :] = moved[WIDTH:] + top * offset[at : at + 1, :]

    tail = pltpu.make_async_remote_copy(
        src_ref=guess.at[:, STEPS - 8 :, :],
        dst_ref=before,
        send_sem=psem.at[0],
        recv_sem=psem.at[1],
        device_id=block(jnp.minimum(place + 1, 127)),
        device_id_type=MESH,
    )

    def to_root(s):
        return pltpu.make_async_remote_copy(
            src_ref=own.at[s],
            dst_ref=ymaps.at[y],
            send_sem=ysend.at[s],
            recv_sem=yrecv.at[y],
            device_id=device(x, c, z, root_at[s]),
            device_id_type=MESH,
        )

    def to_far_root(s):
        return pltpu.make_async_remote_copy(
            src_ref=own.at[s, :HALF],
            dst_ref=ymaps.at[y, :HALF],
            send_sem=ysend.at[0],
            recv_sem=yrecv.at[y],
            device_id=device(x, c, z, (y + 2) % 4),
            device_id_type=MESH,
        )

    def to_relay(s):
        return pltpu.make_async_remote_copy(
            src_ref=own.at[s, HALF:],
            dst_ref=yheld,
            send_sem=ysend.at[1],
            recv_sem=yrelay.at[0],
            device_id=device(x, c, z, (y + 3 - 2 * c) % 4),
            device_id_type=MESH,
        )

    origin = (y + 1 + 2 * c) % 4
    relayed = pltpu.make_async_remote_copy(
        src_ref=yheld,
        dst_ref=ymaps.at[origin, HALF:],
        send_sem=yrelay.at[1],
        recv_sem=yrecv.at[origin],
        device_id=device(x, c, z, (origin + 2) % 4),
        device_id_type=MESH,
    )

    def landed(buffer, sem):
        return pltpu.make_async_remote_copy(
            src_ref=buffer,
            dst_ref=buffer,
            send_sem=sem,
            recv_sem=sem,
            device_id=device(x, c, z, (y + 1) % 4),
            device_id_type=MESH,
        )

    chains(0, 0, SUB // 2)

    one, none = jnp.int32(1), jnp.int32(0)
    sends = jnp.where(place < 127, one, none) + jnp.where(yroot, 4 * one, 2 * one)
    sends = sends + jnp.where(below, one, none) + jnp.where(zroot, 15 * one, none)
    sends = sends + jnp.where(last_z, one, none) + jnp.where(zroot0, one, none) + jnp.where(zroot1 & (x < 3), 2 * one, none)
    pl.semaphore_wait(barrier, sends)


    @pl.when(place < 127)
    def _():
        tail.start()

    chains(0, SUB // 2, SUB)
    chains(1, 0, SUB // 2)

    @pl.when(place > 0)
    def _():
        tail.wait_recv()
        for t in range(2):
            prev[t, 7:8, :] = before[t, 7:8, :]

    @pl.when(place == 0)
    def _():
        for t in range(2):
            prev[t, 7:8, :] = initial[t : t + 1, :]

    earlier = jnp.concatenate([prev[t, 7:15, :] for t in range(2)], axis=0)
    wanted = jnp.concatenate([pre[t * STEPS : t * STEPS + 8, :] for t in range(2)], axis=0)
    steep, added = slopes(earlier, wanted)
    for t in range(2):
        rows = slice(t * 8, t * 8 + 8)
        keep_slopes(slice(t * STEPS, t * STEPS + 8), steep[rows], added[rows])

    for s in range(2):
        if s == 1:
            chains(1, SUB // 2, SUB)
        of_step(start, s * STEPS)
        compose(third, part.at[s, 2], part.at[s, 3])
        compose(first.at[s], start, part.at[s, 0])
        compose(second.at[s], first.at[s], part.at[s, 1])
        compose(own.at[s], second.at[s], third)

        @pl.when(jnp.logical_not(yroot))
        def _():
            to_root(s).start()

        @pl.when(yroot & (mine != s))
        def _():
            to_relay(s).start()
            to_far_root(s).start()

    @pl.when(jnp.logical_not(yroot))
    def _():
        landed(yheld, yrelay.at[0]).wait_recv()
        relayed.start()

    def to_zroot(rows):
        return pltpu.make_async_remote_copy(
            src_ref=ywhole.at[3, rows],
            dst_ref=zmaps.at[z, rows],
            send_sem=zsend.at[0],
            recv_sem=zrecv.at[z],
            device_id=device(x, c, ZROOT, y),
            device_id_type=MESH,
        )

    to_first_z = pltpu.make_async_remote_copy(
        src_ref=ywhole.at[3, HALF:],
        dst_ref=zheld,
        send_sem=zsend.at[1],
        recv_sem=zrelay.at[0],
        device_id=device(x, c, 0, y),
        device_id_type=MESH,
    )
    zrelayed = pltpu.make_async_remote_copy(
        src_ref=zheld,
        dst_ref=zmaps.at[3, HALF:],
        send_sem=zrelay.at[1],
        recv_sem=zrecv.at[3],
        device_id=device(x, c, ZROOT, y),
        device_id_type=MESH,
    )
    near_z = below & (z != 3)

    @pl.when(yroot)
    def _():
        ymaps[y] = own[mine]
        for k in range(4):

            @pl.when(y != k)
            def _():
                landed(ymaps.at[k], yrecv.at[k]).wait_recv()

            if k > 0:
                compose(ywhole.at[k], ymaps.at[0] if k == 1 else ywhole.at[k - 1], ymaps.at[k])

    @pl.when(near_z)
    def _():
        to_zroot(slice(0, ROWS)).start()

    @pl.when(last_z)
    def _():
        to_first_z.start()
        to_zroot(slice(0, HALF)).start()

    def prefix_out(k):
        return pltpu.make_async_remote_copy(
            src_ref=ymaps.at[0] if k == 1 else ywhole.at[k - 1],
            dst_ref=pmaps.at[mine],
            send_sem=fsend.at[k],
            recv_sem=frecv.at[mine],
            device_id=device(x, c, z, k),
            device_id_type=MESH,
        )

    @pl.when(yroot)
    def _():
        for k in range(1, 4):

            @pl.when(y != k)
            def _():
                prefix_out(k).start()

    @pl.when(first_z)
    def _():
        landed(zheld, zrelay.at[0]).wait_recv()
        zrelayed.start()

    across = pltpu.make_async_remote_copy(
        src_ref=zwhole.at[3],
        dst_ref=half,
        send_sem=hsem.at[0],
        recv_sem=hsem.at[1],
        device_id=zroot_id(x, 1),
        device_id_type=MESH,
    )
    across0 = pltpu.make_async_remote_copy(
        src_ref=cout,
        dst_ref=cin,
        send_sem=csem.at[0],
        recv_sem=csem.at[1],
        device_id=zroot_id(x, 1),
        device_id_type=MESH,
    )

    def onward(core):
        return pltpu.make_async_remote_copy(
            src_ref=xout,
            dst_ref=xin,
            send_sem=xsend.at[core],
            recv_sem=xrecv,
            device_id=zroot_id(jnp.minimum(x + 1, 3), core),
            device_id_type=MESH,
        )

    def entry_out(k, at):
        return pltpu.make_async_remote_copy(
            src_ref=zout.at[k],
            dst_ref=fin.at[mine],
            send_sem=esend.at[k * 4 + at],
            recv_sem=erecv.at[mine],
            device_id=device(x, c, k, at),
            device_id_type=MESH,
        )

    def zprefix(k):
        return zmaps.at[0] if k == 0 else zwhole.at[k]

    @pl.when(zroot)
    def _():
        for k in range(4):
            if k != ZROOT:
                landed(zmaps.at[k], zrecv.at[k]).wait_recv()
            if k > 0:
                compose(zwhole.at[k], zprefix(k - 1), ywhole.at[3] if k == ZROOT else zmaps.at[k])

        @pl.when((c == 0) & (x == 0))
        def _():
            given = initial[pl.ds(mine, 1), :]
            ein[...] = tile(given)
            cout[...] = tile(applied(as_columns(given), zwhole.at[3]))
            across0.start()

        @pl.when((c == 0) & (x > 0))
        def _():
            across.start()
            landed(xin, xrecv).wait_recv()
            ein[...] = xin[...]

        @pl.when((c == 1) & (x == 0))
        def _():
            across0.wait_recv()
            ein[...] = cin[...]
            xout[...] = tile(applied(as_columns(cin[0:1, :]), zwhole.at[3]))
            for core in (1, 0):
                onward(core).start()

        @pl.when((c == 1) & (x > 0))
        def _():
            across.wait_recv()
            compose(whole, half, zwhole.at[3])
            landed(xin, xrecv).wait_recv()
            columns = as_columns(xin[0:1, :])

            @pl.when(x < 3)
            def _():
                xout[...] = tile(applied(columns, whole))
                for core in (1, 0):
                    onward(core).start()

            ein[...] = tile(applied(columns, half))

        columns = as_columns(ein[0:1, :])
        for k in range(4):
            zout[k] = ein[...] if k == 0 else tile(applied(columns, zprefix(k - 1)))
            for at in range(4):
                if k != ZROOT:
                    entry_out(k, at).start()
                else:

                    @pl.when(y != at)
                    def _():
                        entry_out(k, at).start()

        fin[mine] = zout[ZROOT]

    for s in range(2):

        @pl.when((y > 0) & (root_at[s] != y))
        def _():
            landed(pmaps.at[s], frecv.at[s]).wait_recv()

    @pl.when(yroot & (y == 1))
    def _():
        pmaps[mine] = ymaps[0]

    for k in range(2, 4):

        @pl.when(yroot & (y == k))
        def _():
            pmaps[mine] = ywhole[k - 1]

    for s in range(2):

        @pl.when(jnp.logical_not(zroot & (mine == s)))
        def _():
            landed(fin.at[s], erecv.at[s]).wait_recv()

        given = fin[s, 0:1, :]
        entries[s] = fin[s]

        @pl.when(y > 0)
        def _():
            entries[s] = tile(applied(as_columns(given), pmaps.at[s]))

    for s in range(2):
        entry = entries[s, 0:1, :]
        columns = as_columns(entry)
        middle = applied(columns, second.at[s])
        at = s * SUBS
        state[at : at + 1, :] = entry
        state[at + 1 : at + 2, :] = applied(columns, first.at[s])
        state[at + 2 : at + 3, :] = middle
        state[at + 3 : at + 4, :] = applied(as_columns(middle), part.at[s, 2])
    now = state[...]
    for inner in range(SUB):
        turned = dot3(now, skew_hi[...], skew_lo[...])
        at = pl.ds(inner, 2 * SUBS, stride=SUB)
        steep = jnp.concatenate([slope2[lanes, at, :] for lanes in range(2)], axis=1)
        added = jnp.concatenate([offset2[lanes, at, :] for lanes in range(2)], axis=1)
        now = keep * now + steep * turned + added
        for lanes in range(2):
            out2[lanes, at, :] = now[:, lanes * 128 : lanes * 128 + 128]
    for lanes in range(2):
        out[:, lanes * 128 : lanes * 128 + 128] = out2[lanes]

    @pl.when(place < 127)
    def _():
        tail.wait_send()

    @pl.when(jnp.logical_not(yroot))
    def _():
        for s in range(2):
            to_root(s).wait_send()
        relayed.wait_send()

    @pl.when(yroot)
    def _():
        to_relay(0).wait_send()
        to_far_root(0).wait_send()

    @pl.when(near_z)
    def _():
        to_zroot(slice(0, ROWS)).wait_send()

    @pl.when(last_z)
    def _():
        to_first_z.wait_send()
        to_zroot(slice(0, HALF)).wait_send()

    @pl.when(first_z)
    def _():
        zrelayed.wait_send()

    @pl.when(zroot0 & (x == 0))
    def _():
        across0.wait_send()

    @pl.when(zroot0 & (x > 0))
    def _():
        across.wait_send()

    @pl.when(zroot1 & (x < 3))
    def _():
        for core in (1, 0):
            onward(core).wait_send()

    @pl.when(zroot)
    def _():
        for k in range(4):
            for at in range(4):
                if k != ZROOT:
                    entry_out(k, at).wait_send()
                else:

                    @pl.when(y != at)
                    def _():
                        entry_out(k, at).wait_send()

    @pl.when(yroot)
    def _():
        for k in range(1, 4):

            @pl.when(y != k)
            def _():
                prefix_out(k).wait_send()


def per_device(guess, inputs, initial, skew_base, in_weight, bias, rate):
    dma = pltpu.SemaphoreType.DMA

    def f32(*shape):
        return pltpu.VMEM(shape, F32)

    maps = (ROWS, WIDTH)
    states = pl.pallas_call(
        kernel,
        out_shape=jax.ShapeDtypeStruct((2 * STEPS, WIDTH), F32),
        in_specs=[pl.BlockSpec(memory_space=pltpu.HBM)] * 7,
        out_specs=pl.BlockSpec(memory_space=pltpu.VMEM),
        scratch_shapes=[
            f32(2, STEPS, WIDTH),
            pltpu.VMEM((2, STEPS, WIDTH), BF16),
            f32(2, WIDTH),
            f32(WIDTH, WIDTH),
            pltpu.VMEM((WIDTH, WIDTH), BF16),
            f32(1, WIDTH),
            f32(1, WIDTH),
            f32(WIDTH, WIDTH),
            pltpu.VMEM((WIDTH, WIDTH), BF16),
            pltpu.VMEM((WIDTH, WIDTH), BF16),
            f32(WIDTH, WIDTH),
            f32(2, 8, WIDTH),
            f32(2, STEPS + 8, WIDTH),
            f32(2 * STEPS, WIDTH),
            f32(2 * STEPS, WIDTH),
            f32(2 * STEPS, WIDTH),
            f32(2, 2 * STEPS, 128),
            f32(2, 2 * STEPS, 128),
            f32(2, 2 * STEPS, 128),
            f32(2, SUBS, *maps),
            f32(*maps),
            f32(2, *maps),
            f32(2, *maps),
            f32(*maps),
            f32(2, *maps),
            f32(4, *maps),
            f32(4, *maps),
            f32(4, *maps),
            f32(4, *maps),
            f32(*maps),
            f32(*maps),
            f32(2, *maps),
            f32(8, WIDTH),
            f32(8, WIDTH),
            f32(8, WIDTH),
            f32(8, WIDTH),
            f32(8, WIDTH),
            f32(4, 8, WIDTH),
            f32(2, 8, WIDTH),
            f32(2, 8, WIDTH),
            f32(8, WIDTH),
            f32(HALF, WIDTH),
            f32(HALF, WIDTH),
            dma((7,)),
            dma((2,)),
            dma((2,)),
            dma((4,)),
            dma((2,)),
            dma((2,)),
            dma((4,)),
            dma((2,)),
            dma((2,)),
            dma((2,)),
            dma((2,)),
            dma,
            dma((16,)),
            dma((2,)),
            dma((4,)),
            dma((2,)),
        ],
        compiler_params=pltpu.CompilerParams(
            collective_id=0, has_side_effects=True, vmem_limit_bytes=60 * 1024 * 1024
        ),
    )(
        guess,
        inputs,
        initial,
        skew_base,
        in_weight,
        bias.reshape(1, WIDTH),
        rate.reshape(1, WIDTH),
    )
    return states.reshape(2, STEPS, WIDTH)


def solution(mesh):
    return jax.shard_map(
        per_device,
        mesh=mesh,
        in_specs=(P(None, SEQ_GRP, None), P(None, SEQ_GRP, None), P(), P(), P(), P(), P()),
        out_specs=P(None, SEQ_GRP, None),
        check_vma=False,
    )
```

```python
import jax
import jax.numpy as jnp
from jax import lax
from jax.experimental import pallas as pl
from jax.experimental.pallas import tpu as pltpu
from jax.sharding import PartitionSpec as P

SEQ_GRP = ("seq", "grp")
MESH = pl.DeviceIdType.MESH
F32 = jnp.float32
BF16 = jnp.bfloat16
GAIN = 0.05

WIDTH = 256
STEPS = 32
SUB = 8
SUBS = STEPS // SUB
ROWS = WIDTH + 16
ZROOT = 3


def split(value):
    high = value.astype(BF16)
    return high, (value - high.astype(F32)).astype(BF16)


def dot(a, b):
    return jnp.dot(a, b, preferred_element_type=F32)


def dot3(value, high, low):
    top, rest = split(value)
    return dot(top, high) + dot(top, low) + dot(rest, high)


def compose(target, left, right):
    high, low = split(right[:WIDTH, :])
    joined = dot3(left[...], high, low)
    target[:WIDTH, :] = joined[:WIDTH]
    target[WIDTH:, :] = joined[WIDTH:] + right[WIDTH:, :]


def as_columns(row):
    turned = jnp.transpose(jnp.broadcast_to(row, (128, WIDTH)))
    return jnp.concatenate([turned, turned], axis=1)


def applied(columns, whole):
    moved = jnp.sum(whole[:WIDTH, :] * columns, axis=0, keepdims=True)
    return moved + whole[WIDTH : WIDTH + 1, :]


def tile(row):
    return jnp.broadcast_to(row, (8, WIDTH))


def kernel(
    guess_in, inputs_in, initial_in, base_in, weight_in, bias_in, rate_in, out,
    guess, inputs, initial, base, weight, bias, rate,
    skew, skew_hi, skew_lo, diag, before, prev, pre, slope, offset, slope2, offset2, out2,
    part, start, first, second, third, own,
    ymaps, ywhole, zmaps, zwhole, half, whole,
    pmaps, xin, cin, ein, xout, cout, zout, fin, entries, state,
    isem, psem, ysend, yrecv, zsend, zrecv, hsem, csem, xsend, xrecv, esend, erecv, fsend, frecv,
):
    seq_at, grp_at = lax.axis_index("seq"), lax.axis_index("grp")
    x, c = seq_at // 2, seq_at % 2
    z, y = grp_at // 4, grp_at % 4
    place = x * 32 + c * 16 + z * 4 + y

    def device(x, c, z, y):
        return (x * 2 + c, z * 4 + y)

    def block(index):
        return (index // 16, index % 16)

    mine = y // 2
    yroot = c == y % 2
    zroot = yroot & (z == ZROOT)
    below = yroot & (z != ZROOT)
    zroot0 = zroot & (c == 0)
    zroot1 = zroot & (c == 1)
    root_at = [2 * s + c for s in range(2)]

    def zroot_id(x, c):
        return device(x, c, ZROOT, 2 * mine + c)

    fetches = [
        pltpu.make_async_copy(source, target, isem.at[index])
        for index, (source, target) in enumerate(
            (
                (guess_in, guess),
                (inputs_in, inputs),
                (initial_in, initial),
                (base_in, base),
                (weight_in, weight),
                (bias_in, bias),
                (rate_in, rate),
            )
        )
    ]
    for index in (3, 6, 0, 1, 4, 5, 2):
        fetches[index].start()

    barrier = pltpu.get_barrier_semaphore()

    def greet(target):
        pl.semaphore_signal(barrier, inc=1, device_id=target, device_id_type=MESH)

    @pl.when(place > 0)
    def _():
        greet(block(place - 1))

    for s in range(2):

        @pl.when(root_at[s] != y)
        def _():
            greet(device(x, c, z, root_at[s]))

    @pl.when(yroot)
    def _():
        for k in range(1, 4):
            greet(device(x, c, z, (y + k) % 4))

    @pl.when(zroot)
    def _():
        for k in range(4):
            if k != ZROOT:
                greet(device(x, c, k, y))

    for s in range(2):

        @pl.when(jnp.logical_not(zroot & (mine == s)))
        def _():
            greet(device(x, c, ZROOT, root_at[s]))

    @pl.when(zroot1)
    def _():
        greet(zroot_id(x, 0))

    @pl.when(zroot & (x > 0))
    def _():
        greet(zroot_id(x - 1, 1))

    fetches[3].wait()
    skew_t = jnp.transpose(base[...]) - base[...]
    skew[...] = skew_t
    high, low = split(skew_t)
    skew_hi[...] = high
    skew_lo[...] = low
    fetches[6].wait()
    keep = 1.0 - rate[...]
    square = (WIDTH, WIDTH)
    eye = lax.broadcasted_iota(jnp.int32, square, 0) == lax.broadcasted_iota(jnp.int32, square, 1)
    diag[...] = jnp.where(eye, jnp.broadcast_to(keep, square), 0.0)
    top = (lax.broadcasted_iota(jnp.int32, (16, WIDTH), 0) == 0).astype(F32)

    fetches[0].wait()
    for s in range(2):
        prev[s, 0:8, :] = jnp.zeros((8, WIDTH), F32)
        prev[s, 8 : 8 + STEPS, :] = guess[s]
    for index in (1, 4, 5, 2):
        fetches[index].wait()
    pre[...] = dot(inputs[...].reshape(2 * STEPS, WIDTH), weight[...]) + bias[...]

    def slopes(earlier, before_tanh):
        lin = dot3(earlier, skew_hi[...], skew_lo[...])
        act = jnp.tanh(lin + before_tanh)
        steep = 1.0 - act * act
        return GAIN * steep, GAIN * (act - steep * lin)

    def keep_slopes(rows, steep, added):
        slope[rows, :] = steep
        offset[rows, :] = added
        for part_at in range(2):
            lanes = slice(part_at * 128, part_at * 128 + 128)
            slope2[part_at, rows, :] = steep[:, lanes]
            offset2[part_at, rows, :] = added[:, lanes]

    earlier = jnp.concatenate([prev[s, 7 : 7 + STEPS, :] for s in range(2)], axis=0)
    keep_slopes(slice(0, 2 * STEPS), *slopes(earlier, pre[...]))

    def of_step(target, at):
        target[:WIDTH, :] = diag[...] + skew[...] * slope[at : at + 1, :]
        target[WIDTH:, :] = top * offset[at : at + 1, :]

    def chains(s, begin, end):
        for inner in range(begin, end):
            if inner == 0:
                for sub in range(SUBS):
                    of_step(part.at[s, sub], s * STEPS + max(sub * SUB, 1))
                continue
            for sub in range(SUBS):
                at = max(sub * SUB, 1) + inner
                if at == SUB * (sub + 1):
                    continue
                at = at + s * STEPS
                held = part[s, sub]
                turned = dot3(held, skew_hi[...], skew_lo[...])
                moved = keep * held + slope[at : at + 1, :] * turned
                part[s, sub, :WIDTH, :] = moved[:WIDTH]
                part[s, sub, WIDTH:, :] = moved[WIDTH:] + top * offset[at : at + 1, :]

    tail = pltpu.make_async_remote_copy(
        src_ref=guess.at[:, STEPS - 8 :, :],
        dst_ref=before,
        send_sem=psem.at[0],
        recv_sem=psem.at[1],
        device_id=block(jnp.minimum(place + 1, 127)),
        device_id_type=MESH,
    )

    def to_root(s):
        return pltpu.make_async_remote_copy(
            src_ref=own.at[s],
            dst_ref=ymaps.at[y],
            send_sem=ysend.at[s],
            recv_sem=yrecv.at[y],
            device_id=device(x, c, z, root_at[s]),
            device_id_type=MESH,
        )

    def landed(buffer, sem):
        return pltpu.make_async_remote_copy(
            src_ref=buffer,
            dst_ref=buffer,
            send_sem=sem,
            recv_sem=sem,
            device_id=device(x, c, z, (y + 1) % 4),
            device_id_type=MESH,
        )

    one, none = jnp.int32(1), jnp.int32(0)
    sends = jnp.where(place < 127, one, none) + jnp.where(yroot, 4 * one, 2 * one)
    sends = sends + jnp.where(below, one, none) + jnp.where(zroot, 15 * one, none)
    sends = sends + jnp.where(zroot0, one, none) + jnp.where(zroot1 & (x < 3), 2 * one, none)
    late = (z == 3) & (y == 3)

    def greeted():
        pl.semaphore_wait(barrier, sends)

        @pl.when(place < 127)
        def _():
            tail.start()

    @pl.when(late)
    def _():
        greeted()

    chains(0, 0, SUB)

    @pl.when(jnp.logical_not(late))
    def _():
        greeted()

    chains(1, 0, SUB // 2)

    @pl.when(place > 0)
    def _():
        tail.wait_recv()
        for t in range(2):
            prev[t, 7:8, :] = before[t, 7:8, :]

    @pl.when(place == 0)
    def _():
        for t in range(2):
            prev[t, 7:8, :] = initial[t : t + 1, :]

    earlier = jnp.concatenate([prev[t, 7:15, :] for t in range(2)], axis=0)
    wanted = jnp.concatenate([pre[t * STEPS : t * STEPS + 8, :] for t in range(2)], axis=0)
    steep, added = slopes(earlier, wanted)
    for t in range(2):
        rows = slice(t * 8, t * 8 + 8)
        keep_slopes(slice(t * STEPS, t * STEPS + 8), steep[rows], added[rows])

    for s in range(2):
        if s == 1:
            chains(1, SUB // 2, SUB)
        of_step(start, s * STEPS)
        compose(third, part.at[s, 2], part.at[s, 3])
        compose(first.at[s], start, part.at[s, 0])
        compose(second.at[s], first.at[s], part.at[s, 1])
        compose(own.at[s], second.at[s], third)

        @pl.when(root_at[s] != y)
        def _():
            to_root(s).start()

    to_zroot = pltpu.make_async_remote_copy(
        src_ref=ywhole.at[3],
        dst_ref=zmaps.at[z],
        send_sem=zsend,
        recv_sem=zrecv.at[z],
        device_id=device(x, c, ZROOT, y),
        device_id_type=MESH,
    )

    @pl.when(yroot)
    def _():
        ymaps[y] = own[mine]
        for k in (2, 3, 0, 1):

            @pl.when(y != k)
            def _():
                landed(ymaps.at[k], yrecv.at[k]).wait_recv()

            if k == 3:
                compose(ywhole.at[0], ymaps.at[2], ymaps.at[3])
        compose(ywhole.at[1], ymaps.at[0], ymaps.at[1])
        compose(ywhole.at[3], ywhole.at[1], ywhole.at[0])

    @pl.when(below)
    def _():
        to_zroot.start()

    def prefix_out(k):
        return pltpu.make_async_remote_copy(
            src_ref=ymaps.at[0] if k == 1 else ywhole.at[k - 1],
            dst_ref=pmaps.at[mine],
            send_sem=fsend.at[k],
            recv_sem=frecv.at[mine],
            device_id=device(x, c, z, k),
            device_id_type=MESH,
        )

    @pl.when(yroot)
    def _():
        compose(ywhole.at[2], ywhole.at[1], ymaps.at[2])
        for k in range(1, 4):

            @pl.when(y != k)
            def _():
                prefix_out(k).start()

    across = pltpu.make_async_remote_copy(
        src_ref=zwhole.at[3],
        dst_ref=half,
        send_sem=hsem.at[0],
        recv_sem=hsem.at[1],
        device_id=zroot_id(x, 1),
        device_id_type=MESH,
    )
    across0 = pltpu.make_async_remote_copy(
        src_ref=cout,
        dst_ref=cin,
        send_sem=csem.at[0],
        recv_sem=csem.at[1],
        device_id=zroot_id(x, 1),
        device_id_type=MESH,
    )

    def onward(core):
        return pltpu.make_async_remote_copy(
            src_ref=xout,
            dst_ref=xin,
            send_sem=xsend.at[core],
            recv_sem=xrecv,
            device_id=zroot_id(jnp.minimum(x + 1, 3), core),
            device_id_type=MESH,
        )

    def entry_out(k, at):
        return pltpu.make_async_remote_copy(
            src_ref=zout.at[k],
            dst_ref=fin.at[mine],
            send_sem=esend.at[k * 4 + at],
            recv_sem=erecv.at[mine],
            device_id=device(x, c, k, at),
            device_id_type=MESH,
        )

    def zprefix(k):
        return zmaps.at[0] if k == 0 else zwhole.at[k]

    @pl.when(zroot)
    def _():
        for k in (2, 0, 1):
            landed(zmaps.at[k], zrecv.at[k]).wait_recv()
            if k == 2:
                compose(zwhole.at[0], zmaps.at[2], ywhole.at[3])
        compose(zwhole.at[1], zmaps.at[0], zmaps.at[1])
        compose(zwhole.at[3], zwhole.at[1], zwhole.at[0])

        @pl.when((c == 0) & (x == 0))
        def _():
            given = initial[pl.ds(mine, 1), :]
            ein[...] = tile(given)
            cout[...] = tile(applied(as_columns(given), zwhole.at[3]))
            across0.start()
            compose(zwhole.at[2], zwhole.at[1], zmaps.at[2])

        @pl.when((c == 0) & (x > 0))
        def _():
            across.start()
            compose(zwhole.at[2], zwhole.at[1], zmaps.at[2])
            landed(xin, xrecv).wait_recv()
            ein[...] = xin[...]

        @pl.when((c == 1) & (x == 0))
        def _():
            compose(zwhole.at[2], zwhole.at[1], zmaps.at[2])
            across0.wait_recv()
            ein[...] = cin[...]
            xout[...] = tile(applied(as_columns(cin[0:1, :]), zwhole.at[3]))
            for core in (1, 0):
                onward(core).start()

        @pl.when((c == 1) & (x > 0))
        def _():
            compose(zwhole.at[2], zwhole.at[1], zmaps.at[2])
            across.wait_recv()
            compose(whole, half, zwhole.at[3])
            landed(xin, xrecv).wait_recv()
            columns = as_columns(xin[0:1, :])

            @pl.when(x < 3)
            def _():
                xout[...] = tile(applied(columns, whole))
                for core in (1, 0):
                    onward(core).start()

            ein[...] = tile(applied(columns, half))

        columns = as_columns(ein[0:1, :])
        for k in range(4):
            zout[k] = ein[...] if k == 0 else tile(applied(columns, zprefix(k - 1)))
            for at in range(4):
                if k != ZROOT:
                    entry_out(k, at).start()
                else:

                    @pl.when(y != at)
                    def _():
                        entry_out(k, at).start()

        fin[mine] = zout[ZROOT]

    for s in range(2):

        @pl.when((y > 0) & (root_at[s] != y))
        def _():
            landed(pmaps.at[s], frecv.at[s]).wait_recv()

    @pl.when(yroot & (y == 1))
    def _():
        pmaps[mine] = ymaps[0]

    for k in range(2, 4):

        @pl.when(yroot & (y == k))
        def _():
            pmaps[mine] = ywhole[k - 1]

    for s in range(2):

        @pl.when(jnp.logical_not(zroot & (mine == s)))
        def _():
            landed(fin.at[s], erecv.at[s]).wait_recv()

        given = fin[s, 0:1, :]
        entries[s] = fin[s]

        @pl.when(y > 0)
        def _():
            entries[s] = tile(applied(as_columns(given), pmaps.at[s]))

    for s in range(2):
        entry = entries[s, 0:1, :]
        columns = as_columns(entry)
        middle = applied(columns, second.at[s])
        at = s * SUBS
        state[at : at + 1, :] = entry
        state[at + 1 : at + 2, :] = applied(columns, first.at[s])
        state[at + 2 : at + 3, :] = middle
        state[at + 3 : at + 4, :] = applied(as_columns(middle), part.at[s, 2])
    now = state[...]
    for inner in range(SUB):
        turned = dot3(now, skew_hi[...], skew_lo[...])
        at = pl.ds(inner, 2 * SUBS, stride=SUB)
        steep = jnp.concatenate([slope2[lanes, at, :] for lanes in range(2)], axis=1)
        added = jnp.concatenate([offset2[lanes, at, :] for lanes in range(2)], axis=1)
        now = keep * now + steep * turned + added
        for lanes in range(2):
            out2[lanes, at, :] = now[:, lanes * 128 : lanes * 128 + 128]
    for lanes in range(2):
        out[:, lanes * 128 : lanes * 128 + 128] = out2[lanes]

    @pl.when(place < 127)
    def _():
        tail.wait_send()

    for s in range(2):

        @pl.when(root_at[s] != y)
        def _():
            to_root(s).wait_send()

    @pl.when(below)
    def _():
        to_zroot.wait_send()

    @pl.when(zroot0 & (x == 0))
    def _():
        across0.wait_send()

    @pl.when(zroot0 & (x > 0))
    def _():
        across.wait_send()

    @pl.when(zroot1 & (x < 3))
    def _():
        for core in (1, 0):
            onward(core).wait_send()

    @pl.when(zroot)
    def _():
        for k in range(4):
            for at in range(4):
                if k != ZROOT:
                    entry_out(k, at).wait_send()
                else:

                    @pl.when(y != at)
                    def _():
                        entry_out(k, at).wait_send()

    @pl.when(yroot)
    def _():
        for k in range(1, 4):

            @pl.when(y != k)
            def _():
                prefix_out(k).wait_send()


def per_device(guess, inputs, initial, skew_base, in_weight, bias, rate):
    dma = pltpu.SemaphoreType.DMA

    def f32(*shape):
        return pltpu.VMEM(shape, F32)

    maps = (ROWS, WIDTH)
    states = pl.pallas_call(
        kernel,
        out_shape=jax.ShapeDtypeStruct((2 * STEPS, WIDTH), F32),
        in_specs=[pl.BlockSpec(memory_space=pltpu.HBM)] * 7,
        out_specs=pl.BlockSpec(memory_space=pltpu.VMEM),
        scratch_shapes=[
            f32(2, STEPS, WIDTH),
            pltpu.VMEM((2, STEPS, WIDTH), BF16),
            f32(2, WIDTH),
            f32(WIDTH, WIDTH),
            pltpu.VMEM((WIDTH, WIDTH), BF16),
            f32(1, WIDTH),
            f32(1, WIDTH),
            f32(WIDTH, WIDTH),
            pltpu.VMEM((WIDTH, WIDTH), BF16),
            pltpu.VMEM((WIDTH, WIDTH), BF16),
            f32(WIDTH, WIDTH),
            f32(2, 8, WIDTH),
            f32(2, STEPS + 8, WIDTH),
            f32(2 * STEPS, WIDTH),
            f32(2 * STEPS, WIDTH),
            f32(2 * STEPS, WIDTH),
            f32(2, 2 * STEPS, 128),
            f32(2, 2 * STEPS, 128),
            f32(2, 2 * STEPS, 128),
            f32(2, SUBS, *maps),
            f32(*maps),
            f32(2, *maps),
            f32(2, *maps),
            f32(*maps),
            f32(2, *maps),
            f32(4, *maps),
            f32(4, *maps),
            f32(4, *maps),
            f32(4, *maps),
            f32(*maps),
            f32(*maps),
            f32(2, *maps),
            f32(8, WIDTH),
            f32(8, WIDTH),
            f32(8, WIDTH),
            f32(8, WIDTH),
            f32(8, WIDTH),
            f32(4, 8, WIDTH),
            f32(2, 8, WIDTH),
            f32(2, 8, WIDTH),
            f32(8, WIDTH),
            dma((7,)),
            dma((2,)),
            dma((2,)),
            dma((4,)),
            dma,
            dma((4,)),
            dma((2,)),
            dma((2,)),
            dma((2,)),
            dma,
            dma((16,)),
            dma((2,)),
            dma((4,)),
            dma((2,)),
        ],
        compiler_params=pltpu.CompilerParams(
            collective_id=0, has_side_effects=True, vmem_limit_bytes=60 * 1024 * 1024
        ),
    )(
        guess,
        inputs,
        initial,
        skew_base,
        in_weight,
        bias.reshape(1, WIDTH),
        rate.reshape(1, WIDTH),
    )
    return states.reshape(2, STEPS, WIDTH)


def solution(mesh):
    return jax.shard_map(
        per_device,
        mesh=mesh,
        in_specs=(P(None, SEQ_GRP, None), P(None, SEQ_GRP, None), P(), P(), P(), P(), P()),
        out_specs=P(None, SEQ_GRP, None),
        check_vma=False,
    )
```

```python
import jax
import jax.numpy as jnp
from jax import lax
from jax.experimental import pallas as pl
from jax.experimental.pallas import tpu as pltpu
from jax.sharding import PartitionSpec as P

SEQ_GRP = ("seq", "grp")
MESH = pl.DeviceIdType.MESH
F32 = jnp.float32
BF16 = jnp.bfloat16
GAIN = 0.05

WIDTH = 256
STEPS = 32
SUB = 8
SUBS = STEPS // SUB
ROWS = WIDTH + 8
ZROOT = 3


def split(value):
    high = value.astype(BF16)
    return high, (value - high.astype(F32)).astype(BF16)


def dot(a, b):
    return jnp.dot(a, b, preferred_element_type=F32)


def dot3(value, high, low):
    top, rest = split(value)
    return dot(top, high) + dot(top, low) + dot(rest, high)


def compose(target, left, right):
    high, low = split(right[:WIDTH, :])
    joined = dot3(left[...], high, low)
    target[:WIDTH, :] = joined[:WIDTH]
    target[WIDTH:, :] = joined[WIDTH:] + right[WIDTH:, :]


def as_columns(row):
    turned = jnp.transpose(jnp.broadcast_to(row, (128, WIDTH)))
    return jnp.concatenate([turned, turned], axis=1)


def applied(columns, whole):
    parts = [
        jnp.sum(whole[at : at + 64, :] * columns[at : at + 64, :], axis=0, keepdims=True)
        for at in range(0, WIDTH, 64)
    ]
    moved = (parts[0] + parts[1]) + (parts[2] + parts[3])
    return moved + whole[WIDTH : WIDTH + 1, :]


def tile(row):
    return jnp.broadcast_to(row, (8, WIDTH))


def kernel(
    guess_in, inputs_in, initial_in, base_in, weight_in, bias_in, rate_in, out,
    guess, inputs, initial, base, weight, bias, rate,
    skew, skew_hi, skew_lo, diag, before, prev, pre, slope, offset, slope2, offset2, out2,
    part, start, first, second, third, own,
    ymaps, ywhole, zmaps, zwhole, half, whole,
    pmaps, xin, cin, ein, xout, cout, zout, fin, entries, state,
    isem, psem, ysend, yrecv, zsend, zrecv, hsem, csem, xsend, xrecv, esend, erecv, fsend, frecv,
):
    seq_at, grp_at = lax.axis_index("seq"), lax.axis_index("grp")
    x, c = seq_at // 2, seq_at % 2
    z, y = grp_at // 4, grp_at % 4
    place = x * 32 + c * 16 + z * 4 + y

    def device(x, c, z, y):
        return (x * 2 + c, z * 4 + y)

    def block(index):
        return (index // 16, index % 16)

    mine = y // 2
    yroot = c == y % 2
    zroot = yroot & (z == ZROOT)
    below = yroot & (z != ZROOT)
    zroot0 = zroot & (c == 0)
    zroot1 = zroot & (c == 1)
    root_at = [2 * s + c for s in range(2)]

    def zroot_id(x, c):
        return device(x, c, ZROOT, 2 * mine + c)

    fetches = [
        pltpu.make_async_copy(source, target, isem.at[index])
        for index, (source, target) in enumerate(
            (
                (guess_in, guess),
                (inputs_in, inputs),
                (initial_in, initial),
                (base_in, base),
                (weight_in, weight),
                (bias_in, bias),
                (rate_in, rate),
            )
        )
    ]
    for index in (3, 6, 0, 1, 4, 5, 2):
        fetches[index].start()

    barrier = pltpu.get_barrier_semaphore()

    def greet(target):
        pl.semaphore_signal(barrier, inc=1, device_id=target, device_id_type=MESH)

    @pl.when(place > 0)
    def _():
        greet(block(place - 1))

    for s in range(2):

        @pl.when(root_at[s] != y)
        def _():
            greet(device(x, c, z, root_at[s]))

    @pl.when(yroot)
    def _():
        for k in range(1, 4):
            greet(device(x, c, z, (y + k) % 4))

    @pl.when(zroot)
    def _():
        for k in range(4):
            if k != ZROOT:
                greet(device(x, c, k, y))

    for s in range(2):

        @pl.when(jnp.logical_not(zroot & (mine == s)))
        def _():
            greet(device(x, c, ZROOT, root_at[s]))

    @pl.when(zroot1)
    def _():
        greet(zroot_id(x, 0))

    @pl.when(zroot & (x > 0))
    def _():
        greet(zroot_id(x - 1, 1))

    fetches[3].wait()
    skew_t = jnp.transpose(base[...]) - base[...]
    skew[...] = skew_t
    high, low = split(skew_t)
    skew_hi[...] = high
    skew_lo[...] = low
    fetches[6].wait()
    keep = 1.0 - rate[...]
    square = (WIDTH, WIDTH)
    eye = lax.broadcasted_iota(jnp.int32, square, 0) == lax.broadcasted_iota(jnp.int32, square, 1)
    diag[...] = jnp.where(eye, jnp.broadcast_to(keep, square), 0.0)
    top = (lax.broadcasted_iota(jnp.int32, (8, WIDTH), 0) == 0).astype(F32)

    fetches[0].wait()
    for s in range(2):
        prev[s, 0:8, :] = jnp.zeros((8, WIDTH), F32)
        prev[s, 8 : 8 + STEPS, :] = guess[s]
    for index in (1, 4, 5, 2):
        fetches[index].wait()
    pre[...] = dot(inputs[...].reshape(2 * STEPS, WIDTH), weight[...]) + bias[...]

    def slopes(earlier, before_tanh):
        lin = dot3(earlier, skew_hi[...], skew_lo[...])
        act = jnp.tanh(lin + before_tanh)
        steep = 1.0 - act * act
        return GAIN * steep, GAIN * (act - steep * lin)

    def keep_slopes(rows, steep, added):
        slope[rows, :] = steep
        offset[rows, :] = added
        for part_at in range(2):
            lanes = slice(part_at * 128, part_at * 128 + 128)
            slope2[part_at, rows, :] = steep[:, lanes]
            offset2[part_at, rows, :] = added[:, lanes]

    earlier = jnp.concatenate([prev[s, 7 : 7 + STEPS, :] for s in range(2)], axis=0)
    keep_slopes(slice(0, 2 * STEPS), *slopes(earlier, pre[...]))

    def of_step(target, at):
        target[:WIDTH, :] = diag[...] + skew[...] * slope[at : at + 1, :]
        target[WIDTH:, :] = top * offset[at : at + 1, :]

    def chains(begin, end):
        for inner in range(begin, end):
            for s in range(2):
                for sub in range(SUBS):
                    first_at = max(sub * SUB, 1)
                    at = first_at + inner
                    if at == SUB * (sub + 1):
                        continue
                    at = at + s * STEPS
                    if inner == 0:
                        of_step(part.at[s, sub], at)
                        continue
                    held = part[s, sub]
                    turned = dot3(held, skew_hi[...], skew_lo[...])
                    moved = keep * held + slope[at : at + 1, :] * turned
                    part[s, sub, :WIDTH, :] = moved[:WIDTH]
                    part[s, sub, WIDTH:, :] = moved[WIDTH:] + top * offset[at : at + 1, :]

    tail = pltpu.make_async_remote_copy(
        src_ref=guess.at[:, STEPS - 8 :, :],
        dst_ref=before,
        send_sem=psem.at[0],
        recv_sem=psem.at[1],
        device_id=block(jnp.minimum(place + 1, 127)),
        device_id_type=MESH,
    )

    def to_root(s):
        return pltpu.make_async_remote_copy(
            src_ref=own.at[s],
            dst_ref=ymaps.at[y],
            send_sem=ysend.at[s],
            recv_sem=yrecv.at[y],
            device_id=device(x, c, z, root_at[s]),
            device_id_type=MESH,
        )

    def landed(buffer, sem):
        return pltpu.make_async_remote_copy(
            src_ref=buffer,
            dst_ref=buffer,
            send_sem=sem,
            recv_sem=sem,
            device_id=device(x, c, z, (y + 1) % 4),
            device_id_type=MESH,
        )

    one, none = jnp.int32(1), jnp.int32(0)
    sends = jnp.where(place < 127, one, none) + jnp.where(yroot, 4 * one, 2 * one)
    sends = sends + jnp.where(below, one, none) + jnp.where(zroot, 15 * one, none)
    sends = sends + jnp.where(zroot0, one, none) + jnp.where(zroot1 & (x < 3), 2 * one, none)
    late = (z == 3) & (y == 3)

    def greeted():
        pl.semaphore_wait(barrier, sends)

        @pl.when(place < 127)
        def _():
            tail.start()

    @pl.when(late)
    def _():
        greeted()

    chains(0, SUB // 2)

    @pl.when(jnp.logical_not(late))
    def _():
        greeted()

    chains(SUB // 2, SUB)

    @pl.when(place > 0)
    def _():
        tail.wait_recv()
        for t in range(2):
            prev[t, 7:8, :] = before[t, 7:8, :]

    @pl.when(place == 0)
    def _():
        for t in range(2):
            prev[t, 7:8, :] = initial[t : t + 1, :]

    earlier = jnp.concatenate([prev[t, 7:15, :] for t in range(2)], axis=0)
    wanted = jnp.concatenate([pre[t * STEPS : t * STEPS + 8, :] for t in range(2)], axis=0)
    steep, added = slopes(earlier, wanted)
    for t in range(2):
        rows = slice(t * 8, t * 8 + 8)
        keep_slopes(slice(t * STEPS, t * STEPS + 8), steep[rows], added[rows])

    for s in range(2):
        of_step(start.at[s], s * STEPS)
        compose(third.at[s], part.at[s, 2], part.at[s, 3])
        compose(first.at[s], start.at[s], part.at[s, 0])
    for s in range(2):
        compose(second.at[s], first.at[s], part.at[s, 1])
    for s in range(2):
        compose(own.at[s], second.at[s], third.at[s])
    for s in range(2):

        @pl.when(root_at[s] != y)
        def _():
            to_root(s).start()

    to_zroot = pltpu.make_async_remote_copy(
        src_ref=ywhole.at[3],
        dst_ref=zmaps.at[z],
        send_sem=zsend,
        recv_sem=zrecv.at[z],
        device_id=device(x, c, ZROOT, y),
        device_id_type=MESH,
    )

    @pl.when(yroot)
    def _():
        ymaps[y] = own[mine]
        for k in (2, 3, 0, 1):

            @pl.when(y != k)
            def _():
                landed(ymaps.at[k], yrecv.at[k]).wait_recv()

            if k == 3:
                compose(ywhole.at[0], ymaps.at[2], ymaps.at[3])
        compose(ywhole.at[1], ymaps.at[0], ymaps.at[1])
        compose(ywhole.at[3], ywhole.at[1], ywhole.at[0])

    @pl.when(below)
    def _():
        to_zroot.start()

    def prefix_out(k):
        return pltpu.make_async_remote_copy(
            src_ref=ymaps.at[0] if k == 1 else ywhole.at[k - 1],
            dst_ref=pmaps.at[mine],
            send_sem=fsend.at[k],
            recv_sem=frecv.at[mine],
            device_id=device(x, c, z, k),
            device_id_type=MESH,
        )

    @pl.when(yroot)
    def _():
        compose(ywhole.at[2], ywhole.at[1], ymaps.at[2])
        for k in range(1, 4):

            @pl.when(y != k)
            def _():
                prefix_out(k).start()

    across = pltpu.make_async_remote_copy(
        src_ref=zwhole.at[3],
        dst_ref=half,
        send_sem=hsem.at[0],
        recv_sem=hsem.at[1],
        device_id=zroot_id(x, 1),
        device_id_type=MESH,
    )
    across0 = pltpu.make_async_remote_copy(
        src_ref=cout,
        dst_ref=cin,
        send_sem=csem.at[0],
        recv_sem=csem.at[1],
        device_id=zroot_id(x, 1),
        device_id_type=MESH,
    )

    def onward(core):
        return pltpu.make_async_remote_copy(
            src_ref=xout,
            dst_ref=xin,
            send_sem=xsend.at[core],
            recv_sem=xrecv,
            device_id=zroot_id(jnp.minimum(x + 1, 3), core),
            device_id_type=MESH,
        )

    def entry_out(k, at):
        return pltpu.make_async_remote_copy(
            src_ref=zout.at[k],
            dst_ref=fin.at[mine],
            send_sem=esend.at[k * 4 + at],
            recv_sem=erecv.at[mine],
            device_id=device(x, c, k, at),
            device_id_type=MESH,
        )

    def zprefix(k):
        return zmaps.at[0] if k == 0 else zwhole.at[k]

    @pl.when(zroot)
    def _():
        for k in (2, 0, 1):
            landed(zmaps.at[k], zrecv.at[k]).wait_recv()
            if k == 2:
                compose(zwhole.at[0], zmaps.at[2], ywhole.at[3])
        compose(zwhole.at[1], zmaps.at[0], zmaps.at[1])
        compose(zwhole.at[3], zwhole.at[1], zwhole.at[0])

        @pl.when((c == 0) & (x == 0))
        def _():
            given = initial[pl.ds(mine, 1), :]
            ein[...] = tile(given)
            cout[...] = tile(applied(as_columns(given), zwhole.at[3]))
            across0.start()
            compose(zwhole.at[2], zwhole.at[1], zmaps.at[2])

        @pl.when((c == 0) & (x > 0))
        def _():
            across.start()
            compose(zwhole.at[2], zwhole.at[1], zmaps.at[2])
            landed(xin, xrecv).wait_recv()
            ein[...] = xin[...]

        @pl.when((c == 1) & (x == 0))
        def _():
            compose(zwhole.at[2], zwhole.at[1], zmaps.at[2])
            across0.wait_recv()
            ein[...] = cin[...]
            xout[...] = tile(applied(as_columns(cin[0:1, :]), zwhole.at[3]))
            for core in (0, 1):
                onward(core).start()

        @pl.when((c == 1) & (x > 0))
        def _():
            compose(zwhole.at[2], zwhole.at[1], zmaps.at[2])
            across.wait_recv()

            @pl.when(x == 2)
            def _():
                compose(whole, half, zwhole.at[3])

            landed(xin, xrecv).wait_recv()
            columns = as_columns(xin[0:1, :])

            @pl.when(x == 2)
            def _():
                xout[...] = tile(applied(columns, whole))
                for core in (0, 1):
                    onward(core).start()

            ein[...] = tile(applied(columns, half))

            @pl.when(x == 1)
            def _():
                xout[...] = tile(applied(as_columns(ein[0:1, :]), zwhole.at[3]))
                for core in (0, 1):
                    onward(core).start()

        columns = as_columns(ein[0:1, :])
        for k in range(4):
            zout[k] = ein[...] if k == 0 else tile(applied(columns, zprefix(k - 1)))
            for at in range(4):
                if k != ZROOT:
                    entry_out(k, at).start()
                else:

                    @pl.when(y != at)
                    def _():
                        entry_out(k, at).start()

        fin[mine] = zout[ZROOT]

    for s in range(2):

        @pl.when((y > 0) & (root_at[s] != y))
        def _():
            landed(pmaps.at[s], frecv.at[s]).wait_recv()

    @pl.when(yroot & (y == 1))
    def _():
        pmaps[mine] = ymaps[0]

    for k in range(2, 4):

        @pl.when(yroot & (y == k))
        def _():
            pmaps[mine] = ywhole[k - 1]

    for s in range(2):

        @pl.when(jnp.logical_not(zroot & (mine == s)))
        def _():
            landed(fin.at[s], erecv.at[s]).wait_recv()

        given = fin[s, 0:1, :]
        entries[s] = fin[s]

        @pl.when(y > 0)
        def _():
            entries[s] = tile(applied(as_columns(given), pmaps.at[s]))

    for s in range(2):
        entry = entries[s, 0:1, :]
        columns = as_columns(entry)
        middle = applied(columns, second.at[s])
        at = s * SUBS
        state[at : at + 1, :] = entry
        state[at + 1 : at + 2, :] = applied(columns, first.at[s])
        state[at + 2 : at + 3, :] = middle
        state[at + 3 : at + 4, :] = applied(as_columns(middle), part.at[s, 2])
    now = state[...]
    for inner in range(SUB):
        turned = dot3(now, skew_hi[...], skew_lo[...])
        at = pl.ds(inner, 2 * SUBS, stride=SUB)
        steep = jnp.concatenate([slope2[lanes, at, :] for lanes in range(2)], axis=1)
        added = jnp.concatenate([offset2[lanes, at, :] for lanes in range(2)], axis=1)
        now = keep * now + steep * turned + added
        for lanes in range(2):
            out2[lanes, at, :] = now[:, lanes * 128 : lanes * 128 + 128]
    for lanes in range(2):
        out[:, lanes * 128 : lanes * 128 + 128] = out2[lanes]

    @pl.when(place < 127)
    def _():
        tail.wait_send()

    for s in range(2):

        @pl.when(root_at[s] != y)
        def _():
            to_root(s).wait_send()

    @pl.when(below)
    def _():
        to_zroot.wait_send()

    @pl.when(zroot0 & (x == 0))
    def _():
        across0.wait_send()

    @pl.when(zroot0 & (x > 0))
    def _():
        across.wait_send()

    @pl.when(zroot1 & (x < 3))
    def _():
        for core in (0, 1):
            onward(core).wait_send()

    @pl.when(zroot)
    def _():
        for k in range(4):
            for at in range(4):
                if k != ZROOT:
                    entry_out(k, at).wait_send()
                else:

                    @pl.when(y != at)
                    def _():
                        entry_out(k, at).wait_send()

    @pl.when(yroot)
    def _():
        for k in range(1, 4):

            @pl.when(y != k)
            def _():
                prefix_out(k).wait_send()


def per_device(guess, inputs, initial, skew_base, in_weight, bias, rate):
    dma = pltpu.SemaphoreType.DMA

    def f32(*shape):
        return pltpu.VMEM(shape, F32)

    maps = (ROWS, WIDTH)
    states = pl.pallas_call(
        kernel,
        out_shape=jax.ShapeDtypeStruct((2 * STEPS, WIDTH), F32),
        in_specs=[pl.BlockSpec(memory_space=pltpu.HBM)] * 7,
        out_specs=pl.BlockSpec(memory_space=pltpu.VMEM),
        scratch_shapes=[
            f32(2, STEPS, WIDTH),
            pltpu.VMEM((2, STEPS, WIDTH), BF16),
            f32(2, WIDTH),
            f32(WIDTH, WIDTH),
            pltpu.VMEM((WIDTH, WIDTH), BF16),
            f32(1, WIDTH),
            f32(1, WIDTH),
            f32(WIDTH, WIDTH),
            pltpu.VMEM((WIDTH, WIDTH), BF16),
            pltpu.VMEM((WIDTH, WIDTH), BF16),
            f32(WIDTH, WIDTH),
            f32(2, 8, WIDTH),
            f32(2, STEPS + 8, WIDTH),
            f32(2 * STEPS, WIDTH),
            f32(2 * STEPS, WIDTH),
            f32(2 * STEPS, WIDTH),
            f32(2, 2 * STEPS, 128),
            f32(2, 2 * STEPS, 128),
            f32(2, 2 * STEPS, 128),
            f32(2, SUBS, *maps),
            f32(2, *maps),
            f32(2, *maps),
            f32(2, *maps),
            f32(2, *maps),
            f32(2, *maps),
            f32(4, *maps),
            f32(4, *maps),
            f32(4, *maps),
            f32(4, *maps),
            f32(*maps),
            f32(*maps),
            f32(2, *maps),
            f32(8, WIDTH),
            f32(8, WIDTH),
            f32(8, WIDTH),
            f32(8, WIDTH),
            f32(8, WIDTH),
            f32(4, 8, WIDTH),
            f32(2, 8, WIDTH),
            f32(2, 8, WIDTH),
            f32(8, WIDTH),
            dma((7,)),
            dma((2,)),
            dma((2,)),
            dma((4,)),
            dma,
            dma((4,)),
            dma((2,)),
            dma((2,)),
            dma((2,)),
            dma,
            dma((16,)),
            dma((2,)),
            dma((4,)),
            dma((2,)),
        ],
        compiler_params=pltpu.CompilerParams(
            collective_id=0, has_side_effects=True, vmem_limit_bytes=60 * 1024 * 1024
        ),
    )(
        guess,
        inputs,
        initial,
        skew_base,
        in_weight,
        bias.reshape(1, WIDTH),
        rate.reshape(1, WIDTH),
    )
    return states.reshape(2, STEPS, WIDTH)


def solution(mesh):
    return jax.shard_map(
        per_device,
        mesh=mesh,
        in_specs=(P(None, SEQ_GRP, None), P(None, SEQ_GRP, None), P(), P(), P(), P(), P()),
        out_specs=P(None, SEQ_GRP, None),
        check_vma=False,
    )
```

```python
import jax
import jax.numpy as jnp
from jax import lax
from jax.experimental import pallas as pl
from jax.experimental.pallas import tpu as pltpu
from jax.sharding import PartitionSpec as P

SEQ_GRP = ("seq", "grp")
MESH = pl.DeviceIdType.MESH
F32 = jnp.float32
BF16 = jnp.bfloat16
GAIN = 0.05

WIDTH = 256
STEPS = 32
SUB = 8
SUBS = STEPS // SUB
ROWS = WIDTH + 8
ZROOT = 3


def split(value):
    high = value.astype(BF16)
    return high, (value - high.astype(F32)).astype(BF16)


def dot(a, b):
    return jnp.dot(a, b, preferred_element_type=F32)


def dot3(value, high, low):
    top, rest = split(value)
    return dot(top, high) + dot(top, low) + dot(rest, high)


def compose(target, left, right):
    high, low = split(right[:WIDTH, :])
    joined = dot3(left[...], high, low)
    target[:WIDTH, :] = joined[:WIDTH]
    target[WIDTH:, :] = joined[WIDTH:] + right[WIDTH:, :]


def as_columns(row):
    turned = jnp.transpose(jnp.broadcast_to(row, (128, WIDTH)))
    return jnp.concatenate([turned, turned], axis=1)


def applied(columns, whole):
    parts = [
        jnp.sum(whole[at : at + 64, :] * columns[at : at + 64, :], axis=0, keepdims=True)
        for at in range(0, WIDTH, 64)
    ]
    moved = (parts[0] + parts[1]) + (parts[2] + parts[3])
    return moved + whole[WIDTH : WIDTH + 1, :]


def tile(row):
    return jnp.broadcast_to(row, (8, WIDTH))


def kernel(
    guess_in, inputs_in, initial_in, base_in, weight_in, bias_in, rate_in, out,
    guess, inputs, initial, base, weight, bias, rate,
    skew, skew_hi, skew_lo, diag, before, prev, pre, slope, offset, slope2, offset2, out2,
    part, start, first, second, third, own,
    ymaps, ywhole, zmaps, zwhole, half, whole,
    pmaps, xin, cin, ein, xout, cout, zout, fin, entries, state,
    isem, psem, ysend, yrecv, zsend, zrecv, hsem, csem, xsend, xrecv, esend, erecv, fsend, frecv,
):
    seq_at, grp_at = lax.axis_index("seq"), lax.axis_index("grp")
    x, c = seq_at // 2, seq_at % 2
    z, y = grp_at // 4, grp_at % 4
    place = x * 32 + c * 16 + z * 4 + y

    def device(x, c, z, y):
        return (x * 2 + c, z * 4 + y)

    def block(index):
        return (index // 16, index % 16)

    mine = y // 2
    yroot = c == y % 2
    zroot = yroot & (z == ZROOT)
    below = yroot & (z != ZROOT)
    zroot0 = zroot & (c == 0)
    zroot1 = zroot & (c == 1)
    root_at = [2 * s + c for s in range(2)]

    def zroot_id(x, c):
        return device(x, c, ZROOT, 2 * mine + c)

    fetches = [
        pltpu.make_async_copy(source, target, isem.at[index])
        for index, (source, target) in enumerate(
            (
                (guess_in, guess),
                (inputs_in, inputs),
                (initial_in, initial),
                (base_in, base),
                (weight_in, weight),
                (bias_in, bias),
                (rate_in, rate),
            )
        )
    ]
    for index in (3, 6, 0, 1, 4, 5, 2):
        fetches[index].start()

    barrier = pltpu.get_barrier_semaphore()

    def greet(target):
        pl.semaphore_signal(barrier, inc=1, device_id=target, device_id_type=MESH)

    @pl.when(place > 0)
    def _():
        greet(block(place - 1))

    for s in range(2):

        @pl.when(root_at[s] != y)
        def _():
            greet(device(x, c, z, root_at[s]))

    @pl.when(yroot)
    def _():
        for k in range(1, 4):
            greet(device(x, c, z, (y + k) % 4))

    @pl.when(zroot)
    def _():
        for k in range(4):
            if k != ZROOT:
                greet(device(x, c, k, y))

    for s in range(2):

        @pl.when(jnp.logical_not(zroot & (mine == s)))
        def _():
            greet(device(x, c, ZROOT, root_at[s]))

    @pl.when(zroot1)
    def _():
        greet(zroot_id(x, 0))

    inner_slab = (x == 1) | (x == 2)

    @pl.when(zroot0 & inner_slab)
    def _():
        greet(zroot_id(x, 1))

    @pl.when(zroot & (x > 0))
    def _():
        greet(zroot_id(x - 1, jnp.where(x == 1, 1, c)))

    fetches[3].wait()
    skew_t = jnp.transpose(base[...]) - base[...]
    skew[...] = skew_t
    high, low = split(skew_t)
    skew_hi[...] = high
    skew_lo[...] = low
    fetches[6].wait()
    keep = 1.0 - rate[...]
    square = (WIDTH, WIDTH)
    eye = lax.broadcasted_iota(jnp.int32, square, 0) == lax.broadcasted_iota(jnp.int32, square, 1)
    diag[...] = jnp.where(eye, jnp.broadcast_to(keep, square), 0.0)
    top = (lax.broadcasted_iota(jnp.int32, (8, WIDTH), 0) == 0).astype(F32)

    fetches[0].wait()
    for s in range(2):
        prev[s, 0:8, :] = jnp.zeros((8, WIDTH), F32)
        prev[s, 8 : 8 + STEPS, :] = guess[s]
    for index in (1, 4, 5, 2):
        fetches[index].wait()
    pre[...] = dot(inputs[...].reshape(2 * STEPS, WIDTH), weight[...]) + bias[...]

    def slopes(earlier, before_tanh):
        lin = dot3(earlier, skew_hi[...], skew_lo[...])
        act = jnp.tanh(lin + before_tanh)
        steep = 1.0 - act * act
        return GAIN * steep, GAIN * (act - steep * lin)

    def keep_slopes(rows, steep, added):
        slope[rows, :] = steep
        offset[rows, :] = added
        for part_at in range(2):
            lanes = slice(part_at * 128, part_at * 128 + 128)
            slope2[part_at, rows, :] = steep[:, lanes]
            offset2[part_at, rows, :] = added[:, lanes]

    earlier = jnp.concatenate([prev[s, 7 : 7 + STEPS, :] for s in range(2)], axis=0)
    keep_slopes(slice(0, 2 * STEPS), *slopes(earlier, pre[...]))

    def of_step(target, at):
        target[:WIDTH, :] = diag[...] + skew[...] * slope[at : at + 1, :]
        target[WIDTH:, :] = top * offset[at : at + 1, :]

    def chains(begin, end):
        for inner in range(begin, end):
            for s in range(2):
                for sub in range(SUBS):
                    first_at = max(sub * SUB, 1)
                    at = first_at + inner
                    if at == SUB * (sub + 1):
                        continue
                    at = at + s * STEPS
                    if inner == 0:
                        of_step(part.at[s, sub], at)
                        continue
                    held = part[s, sub]
                    turned = dot3(held, skew_hi[...], skew_lo[...])
                    moved = keep * held + slope[at : at + 1, :] * turned
                    part[s, sub, :WIDTH, :] = moved[:WIDTH]
                    part[s, sub, WIDTH:, :] = moved[WIDTH:] + top * offset[at : at + 1, :]

    tail = pltpu.make_async_remote_copy(
        src_ref=guess.at[:, STEPS - 8 :, :],
        dst_ref=before,
        send_sem=psem.at[0],
        recv_sem=psem.at[1],
        device_id=block(jnp.minimum(place + 1, 127)),
        device_id_type=MESH,
    )

    def to_root(s):
        return pltpu.make_async_remote_copy(
            src_ref=own.at[s],
            dst_ref=ymaps.at[y],
            send_sem=ysend.at[s],
            recv_sem=yrecv.at[y],
            device_id=device(x, c, z, root_at[s]),
            device_id_type=MESH,
        )

    def landed(buffer, sem):
        return pltpu.make_async_remote_copy(
            src_ref=buffer,
            dst_ref=buffer,
            send_sem=sem,
            recv_sem=sem,
            device_id=device(x, c, z, (y + 1) % 4),
            device_id_type=MESH,
        )

    one, none = jnp.int32(1), jnp.int32(0)
    sends = jnp.where(place < 127, one, none) + jnp.where(yroot, 4 * one, 2 * one)
    sends = sends + jnp.where(below, one, none) + jnp.where(zroot, 15 * one, none)
    sends = sends + jnp.where(zroot0, one, none) + jnp.where(zroot1 & (x == 0), 2 * one, none)
    sends = sends + jnp.where(zroot & inner_slab, one, none)
    sends = sends + jnp.where(zroot1 & inner_slab, one, none)
    late = (z == 3) & (y == 3)

    def greeted():
        pl.semaphore_wait(barrier, sends)

        @pl.when(place < 127)
        def _():
            tail.start()

    @pl.when(late)
    def _():
        greeted()

    chains(0, SUB // 2)

    @pl.when(jnp.logical_not(late))
    def _():
        greeted()

    chains(SUB // 2, SUB)

    @pl.when(place > 0)
    def _():
        tail.wait_recv()
        for t in range(2):
            prev[t, 7:8, :] = before[t, 7:8, :]

    @pl.when(place == 0)
    def _():
        for t in range(2):
            prev[t, 7:8, :] = initial[t : t + 1, :]

    earlier = jnp.concatenate([prev[t, 7:15, :] for t in range(2)], axis=0)
    wanted = jnp.concatenate([pre[t * STEPS : t * STEPS + 8, :] for t in range(2)], axis=0)
    steep, added = slopes(earlier, wanted)
    for t in range(2):
        rows = slice(t * 8, t * 8 + 8)
        keep_slopes(slice(t * STEPS, t * STEPS + 8), steep[rows], added[rows])

    for s in range(2):
        of_step(start.at[s], s * STEPS)
        compose(third.at[s], part.at[s, 2], part.at[s, 3])
        compose(first.at[s], start.at[s], part.at[s, 0])
    for s in range(2):
        compose(second.at[s], first.at[s], part.at[s, 1])
    for s in range(2):
        compose(own.at[s], second.at[s], third.at[s])
    for s in range(2):

        @pl.when(root_at[s] != y)
        def _():
            to_root(s).start()

    to_zroot = pltpu.make_async_remote_copy(
        src_ref=ywhole.at[3],
        dst_ref=zmaps.at[z],
        send_sem=zsend,
        recv_sem=zrecv.at[z],
        device_id=device(x, c, ZROOT, y),
        device_id_type=MESH,
    )

    @pl.when(yroot)
    def _():
        ymaps[y] = own[mine]
        for k in (2, 3, 0, 1):

            @pl.when(y != k)
            def _():
                landed(ymaps.at[k], yrecv.at[k]).wait_recv()

            if k == 3:
                compose(ywhole.at[0], ymaps.at[2], ymaps.at[3])
        compose(ywhole.at[1], ymaps.at[0], ymaps.at[1])
        compose(ywhole.at[3], ywhole.at[1], ywhole.at[0])

    @pl.when(below)
    def _():
        to_zroot.start()

    def prefix_out(k):
        return pltpu.make_async_remote_copy(
            src_ref=ymaps.at[0] if k == 1 else ywhole.at[k - 1],
            dst_ref=pmaps.at[mine],
            send_sem=fsend.at[k],
            recv_sem=frecv.at[mine],
            device_id=device(x, c, z, k),
            device_id_type=MESH,
        )

    @pl.when(yroot)
    def _():
        compose(ywhole.at[2], ywhole.at[1], ymaps.at[2])
        for k in range(1, 4):

            @pl.when(y != k)
            def _():
                prefix_out(k).start()

    across = pltpu.make_async_remote_copy(
        src_ref=zwhole.at[3],
        dst_ref=half,
        send_sem=hsem.at[0],
        recv_sem=hsem.at[1],
        device_id=zroot_id(x, 1),
        device_id_type=MESH,
    )
    back = pltpu.make_async_remote_copy(
        src_ref=zwhole.at[3],
        dst_ref=half,
        send_sem=hsem.at[0],
        recv_sem=hsem.at[1],
        device_id=zroot_id(x, 0),
        device_id_type=MESH,
    )
    across0 = pltpu.make_async_remote_copy(
        src_ref=cout,
        dst_ref=cin,
        send_sem=csem.at[0],
        recv_sem=csem.at[1],
        device_id=zroot_id(x, 1),
        device_id_type=MESH,
    )

    def onward(core):
        return pltpu.make_async_remote_copy(
            src_ref=xout,
            dst_ref=xin,
            send_sem=xsend.at[core],
            recv_sem=xrecv,
            device_id=zroot_id(jnp.minimum(x + 1, 3), core),
            device_id_type=MESH,
        )

    def entry_out(k, at):
        return pltpu.make_async_remote_copy(
            src_ref=zout.at[k],
            dst_ref=fin.at[mine],
            send_sem=esend.at[k * 4 + at],
            recv_sem=erecv.at[mine],
            device_id=device(x, c, k, at),
            device_id_type=MESH,
        )

    def zprefix(k):
        return zmaps.at[0] if k == 0 else zwhole.at[k]

    @pl.when(zroot)
    def _():
        for k in (2, 0, 1):
            landed(zmaps.at[k], zrecv.at[k]).wait_recv()
            if k == 2:
                compose(zwhole.at[0], zmaps.at[2], ywhole.at[3])
        compose(zwhole.at[1], zmaps.at[0], zmaps.at[1])
        compose(zwhole.at[3], zwhole.at[1], zwhole.at[0])

        @pl.when((c == 0) & (x == 0))
        def _():
            given = initial[pl.ds(mine, 1), :]
            ein[...] = tile(given)
            cout[...] = tile(applied(as_columns(given), zwhole.at[3]))
            across0.start()
            compose(zwhole.at[2], zwhole.at[1], zmaps.at[2])

        @pl.when((c == 0) & (x > 0))
        def _():
            across.start()
            compose(zwhole.at[2], zwhole.at[1], zmaps.at[2])

            @pl.when(x < 3)
            def _():
                landed(half, hsem.at[1]).wait_recv()
                compose(whole, zwhole.at[3], half)

            landed(xin, xrecv).wait_recv()
            ein[...] = xin[...]

            @pl.when(x < 3)
            def _():
                xout[...] = tile(applied(as_columns(xin[0:1, :]), whole))
                onward(0).start()


        @pl.when((c == 1) & (x == 0))
        def _():
            compose(zwhole.at[2], zwhole.at[1], zmaps.at[2])
            across0.wait_recv()
            ein[...] = cin[...]
            xout[...] = tile(applied(as_columns(cin[0:1, :]), zwhole.at[3]))
            for core in (0, 1):
                onward(core).start()

        @pl.when((c == 1) & (x > 0))
        def _():
            @pl.when(x < 3)
            def _():
                back.start()

            compose(zwhole.at[2], zwhole.at[1], zmaps.at[2])
            across.wait_recv()

            @pl.when(x == 2)
            def _():
                compose(whole, half, zwhole.at[3])

            landed(xin, xrecv).wait_recv()
            columns = as_columns(xin[0:1, :])

            @pl.when(x == 2)
            def _():
                xout[...] = tile(applied(columns, whole))
                onward(1).start()

            ein[...] = tile(applied(columns, half))

            @pl.when(x == 1)
            def _():
                xout[...] = tile(applied(as_columns(ein[0:1, :]), zwhole.at[3]))
                onward(1).start()

        columns = as_columns(ein[0:1, :])
        for k in range(4):
            zout[k] = ein[...] if k == 0 else tile(applied(columns, zprefix(k - 1)))
            for at in range(4):
                if k != ZROOT:
                    entry_out(k, at).start()
                else:

                    @pl.when(y != at)
                    def _():
                        entry_out(k, at).start()

        fin[mine] = zout[ZROOT]

    for s in range(2):

        @pl.when((y > 0) & (root_at[s] != y))
        def _():
            landed(pmaps.at[s], frecv.at[s]).wait_recv()

    @pl.when(yroot & (y == 1))
    def _():
        pmaps[mine] = ymaps[0]

    for k in range(2, 4):

        @pl.when(yroot & (y == k))
        def _():
            pmaps[mine] = ywhole[k - 1]

    for s in range(2):

        @pl.when(jnp.logical_not(zroot & (mine == s)))
        def _():
            landed(fin.at[s], erecv.at[s]).wait_recv()

        given = fin[s, 0:1, :]
        entries[s] = fin[s]

        @pl.when(y > 0)
        def _():
            entries[s] = tile(applied(as_columns(given), pmaps.at[s]))

    for s in range(2):
        entry = entries[s, 0:1, :]
        columns = as_columns(entry)
        middle = applied(columns, second.at[s])
        at = s * SUBS
        state[at : at + 1, :] = entry
        state[at + 1 : at + 2, :] = applied(columns, first.at[s])
        state[at + 2 : at + 3, :] = middle
        state[at + 3 : at + 4, :] = applied(as_columns(middle), part.at[s, 2])
    now = state[...]
    for inner in range(SUB):
        turned = dot3(now, skew_hi[...], skew_lo[...])
        at = pl.ds(inner, 2 * SUBS, stride=SUB)
        steep = jnp.concatenate([slope2[lanes, at, :] for lanes in range(2)], axis=1)
        added = jnp.concatenate([offset2[lanes, at, :] for lanes in range(2)], axis=1)
        now = keep * now + steep * turned + added
        for lanes in range(2):
            out2[lanes, at, :] = now[:, lanes * 128 : lanes * 128 + 128]
    for lanes in range(2):
        out[:, lanes * 128 : lanes * 128 + 128] = out2[lanes]

    @pl.when(place < 127)
    def _():
        tail.wait_send()

    for s in range(2):

        @pl.when(root_at[s] != y)
        def _():
            to_root(s).wait_send()

    @pl.when(below)
    def _():
        to_zroot.wait_send()

    @pl.when(zroot0 & (x == 0))
    def _():
        across0.wait_send()

    @pl.when(zroot0 & (x > 0))
    def _():
        across.wait_send()

    @pl.when(zroot1 & inner_slab)
    def _():
        back.wait_send()

    @pl.when(zroot1 & (x < 3))
    def _():
        onward(1).wait_send()

    @pl.when((zroot1 & (x == 0)) | (zroot0 & inner_slab))
    def _():
        onward(0).wait_send()

    @pl.when(zroot)
    def _():
        for k in range(4):
            for at in range(4):
                if k != ZROOT:
                    entry_out(k, at).wait_send()
                else:

                    @pl.when(y != at)
                    def _():
                        entry_out(k, at).wait_send()

    @pl.when(yroot)
    def _():
        for k in range(1, 4):

            @pl.when(y != k)
            def _():
                prefix_out(k).wait_send()


def per_device(guess, inputs, initial, skew_base, in_weight, bias, rate):
    dma = pltpu.SemaphoreType.DMA

    def f32(*shape):
        return pltpu.VMEM(shape, F32)

    maps = (ROWS, WIDTH)
    states = pl.pallas_call(
        kernel,
        out_shape=jax.ShapeDtypeStruct((2 * STEPS, WIDTH), F32),
        in_specs=[pl.BlockSpec(memory_space=pltpu.HBM)] * 7,
        out_specs=pl.BlockSpec(memory_space=pltpu.VMEM),
        scratch_shapes=[
            f32(2, STEPS, WIDTH),
            pltpu.VMEM((2, STEPS, WIDTH), BF16),
            f32(2, WIDTH),
            f32(WIDTH, WIDTH),
            pltpu.VMEM((WIDTH, WIDTH), BF16),
            f32(1, WIDTH),
            f32(1, WIDTH),
            f32(WIDTH, WIDTH),
            pltpu.VMEM((WIDTH, WIDTH), BF16),
            pltpu.VMEM((WIDTH, WIDTH), BF16),
            f32(WIDTH, WIDTH),
            f32(2, 8, WIDTH),
            f32(2, STEPS + 8, WIDTH),
            f32(2 * STEPS, WIDTH),
            f32(2 * STEPS, WIDTH),
            f32(2 * STEPS, WIDTH),
            f32(2, 2 * STEPS, 128),
            f32(2, 2 * STEPS, 128),
            f32(2, 2 * STEPS, 128),
            f32(2, SUBS, *maps),
            f32(2, *maps),
            f32(2, *maps),
            f32(2, *maps),
            f32(2, *maps),
            f32(2, *maps),
            f32(4, *maps),
            f32(4, *maps),
            f32(4, *maps),
            f32(4, *maps),
            f32(*maps),
            f32(*maps),
            f32(2, *maps),
            f32(8, WIDTH),
            f32(8, WIDTH),
            f32(8, WIDTH),
            f32(8, WIDTH),
            f32(8, WIDTH),
            f32(4, 8, WIDTH),
            f32(2, 8, WIDTH),
            f32(2, 8, WIDTH),
            f32(8, WIDTH),
            dma((7,)),
            dma((2,)),
            dma((2,)),
            dma((4,)),
            dma,
            dma((4,)),
            dma((2,)),
            dma((2,)),
            dma((2,)),
            dma,
            dma((16,)),
            dma((2,)),
            dma((4,)),
            dma((2,)),
        ],
        compiler_params=pltpu.CompilerParams(
            collective_id=0, has_side_effects=True, vmem_limit_bytes=60 * 1024 * 1024
        ),
    )(
        guess,
        inputs,
        initial,
        skew_base,
        in_weight,
        bias.reshape(1, WIDTH),
        rate.reshape(1, WIDTH),
    )
    return states.reshape(2, STEPS, WIDTH)


def solution(mesh):
    return jax.shard_map(
        per_device,
        mesh=mesh,
        in_specs=(P(None, SEQ_GRP, None), P(None, SEQ_GRP, None), P(), P(), P(), P(), P()),
        out_specs=P(None, SEQ_GRP, None),
        check_vma=False,
    )
```

```python
import jax
import jax.numpy as jnp
from jax import lax
from jax.experimental import pallas as pl
from jax.experimental.pallas import tpu as pltpu
from jax.sharding import PartitionSpec as P

SEQ_GRP = ("seq", "grp")
MESH = pl.DeviceIdType.MESH
F32 = jnp.float32
BF16 = jnp.bfloat16
GAIN = 0.05

WIDTH = 256
STEPS = 32
SUB = 8
SUBS = STEPS // SUB
ROWS = WIDTH + 8
ZROOT = 3


def split(value):
    high = value.astype(BF16)
    return high, (value - high.astype(F32)).astype(BF16)


def dot(a, b):
    return jnp.dot(a, b, preferred_element_type=F32)


def dot3(value, high, low):
    top, rest = split(value)
    return dot(top, high) + dot(top, low) + dot(rest, high)


def compose(target, left, right):
    high, low = split(right[:WIDTH, :])
    joined = dot3(left[...], high, low)
    target[:WIDTH, :] = joined[:WIDTH]
    target[WIDTH:, :] = joined[WIDTH:] + right[WIDTH:, :]


def as_columns(row):
    turned = jnp.transpose(jnp.broadcast_to(row, (128, WIDTH)))
    return jnp.concatenate([turned, turned], axis=1)


def applied(columns, whole):
    parts = [
        jnp.sum(whole[at : at + 64, :] * columns[at : at + 64, :], axis=0, keepdims=True)
        for at in range(0, WIDTH, 64)
    ]
    moved = (parts[0] + parts[1]) + (parts[2] + parts[3])
    return moved + whole[WIDTH : WIDTH + 1, :]


def tile(row):
    return jnp.broadcast_to(row, (8, WIDTH))


def kernel(
    guess_in, inputs_in, initial_in, base_in, weight_in, bias_in, rate_in, out,
    guess, inputs, initial, base, weight, bias, rate,
    skew, skew_hi, skew_lo, diag, before, prev, pre, slope, offset, slope2, offset2, out2,
    part, start, first, second, third, own,
    ymaps, ywhole, zmaps, zwhole, half, whole,
    pmaps, xin, cin, ein, xout, cout, zout, fin, entries, state,
    isem, psem, ysend, yrecv, zsend, zrecv, hsem, csem, xsend, xrecv, esend, erecv, fsend, frecv,
):
    seq_at, grp_at = lax.axis_index("seq"), lax.axis_index("grp")
    x, c = seq_at // 2, seq_at % 2
    z, y = grp_at // 4, grp_at % 4
    place = x * 32 + c * 16 + z * 4 + y

    def device(x, c, z, y):
        return (x * 2 + c, z * 4 + y)

    def block(index):
        return (index // 16, index % 16)

    mine = y // 2
    yroot = c == y % 2
    zroot = yroot & (z == ZROOT)
    below = yroot & (z != ZROOT)
    zroot0 = zroot & (c == 0)
    zroot1 = zroot & (c == 1)
    root_at = [2 * s + c for s in range(2)]

    def zroot_id(x, c):
        return device(x, c, ZROOT, 2 * mine + c)

    fetches = [
        pltpu.make_async_copy(source, target, isem.at[index])
        for index, (source, target) in enumerate(
            (
                (guess_in, guess),
                (inputs_in, inputs),
                (initial_in, initial),
                (base_in, base),
                (weight_in, weight),
                (bias_in, bias),
                (rate_in, rate),
            )
        )
    ]
    for index in (3, 6, 0, 1, 4, 5, 2):
        fetches[index].start()

    barrier = pltpu.get_barrier_semaphore()

    def greet(target):
        pl.semaphore_signal(barrier, inc=1, device_id=target, device_id_type=MESH)

    @pl.when(place > 0)
    def _():
        greet(block(place - 1))

    for s in range(2):

        @pl.when(root_at[s] != y)
        def _():
            greet(device(x, c, z, root_at[s]))

    @pl.when(yroot)
    def _():
        for k in range(1, 4):
            greet(device(x, c, z, (y + k) % 4))

    @pl.when(zroot)
    def _():
        for k in range(4):
            if k != ZROOT:
                greet(device(x, c, k, y))

    for s in range(2):

        @pl.when(jnp.logical_not(zroot & (mine == s)))
        def _():
            greet(device(x, c, ZROOT, root_at[s]))

    @pl.when(zroot1)
    def _():
        greet(zroot_id(x, 0))

    inner_slab = (x == 1) | (x == 2)

    @pl.when(zroot0 & inner_slab)
    def _():
        greet(zroot_id(x, 1))

    @pl.when(zroot & (x > 0))
    def _():
        greet(zroot_id(x - 1, jnp.where(x == 1, 1, c)))

    fetches[3].wait()
    skew_t = jnp.transpose(base[...]) - base[...]
    skew[...] = skew_t
    high, low = split(skew_t)
    skew_hi[...] = high
    skew_lo[...] = low
    fetches[6].wait()
    keep = 1.0 - rate[...]
    square = (WIDTH, WIDTH)
    eye = lax.broadcasted_iota(jnp.int32, square, 0) == lax.broadcasted_iota(jnp.int32, square, 1)
    diag[...] = jnp.where(eye, jnp.broadcast_to(keep, square), 0.0)
    top = (lax.broadcasted_iota(jnp.int32, (8, WIDTH), 0) == 0).astype(F32)

    fetches[0].wait()
    for s in range(2):
        prev[s, 0:8, :] = jnp.zeros((8, WIDTH), F32)
        prev[s, 8 : 8 + STEPS, :] = guess[s]
    for index in (1, 4, 5, 2):
        fetches[index].wait()
    pre[...] = dot(inputs[...].reshape(2 * STEPS, WIDTH), weight[...]) + bias[...]

    def slopes(earlier, before_tanh):
        lin = dot3(earlier, skew_hi[...], skew_lo[...])
        act = jnp.tanh(lin + before_tanh)
        steep = 1.0 - act * act
        return GAIN * steep, GAIN * (act - steep * lin)

    def keep_slopes(rows, steep, added):
        slope[rows, :] = steep
        offset[rows, :] = added
        for part_at in range(2):
            lanes = slice(part_at * 128, part_at * 128 + 128)
            slope2[part_at, rows, :] = steep[:, lanes]
            offset2[part_at, rows, :] = added[:, lanes]

    earlier = jnp.concatenate([prev[s, 7 : 7 + STEPS, :] for s in range(2)], axis=0)
    keep_slopes(slice(0, 2 * STEPS), *slopes(earlier, pre[...]))

    def of_step(target, at):
        target[:WIDTH, :] = diag[...] + skew[...] * slope[at : at + 1, :]
        target[WIDTH:, :] = top * offset[at : at + 1, :]

    def chains(begin, end):
        for inner in range(begin, end):
            for s in range(2):
                for sub in range(SUBS):
                    first_at = max(sub * SUB, 1)
                    at = first_at + inner
                    if at == SUB * (sub + 1):
                        continue
                    at = at + s * STEPS
                    if inner == 0:
                        of_step(part.at[s, sub], at)
                        continue
                    held = part[s, sub]
                    turned = dot3(held, skew_hi[...], skew_lo[...])
                    moved = keep * held + slope[at : at + 1, :] * turned
                    part[s, sub, :WIDTH, :] = moved[:WIDTH]
                    part[s, sub, WIDTH:, :] = moved[WIDTH:] + top * offset[at : at + 1, :]

    tail = pltpu.make_async_remote_copy(
        src_ref=guess.at[:, STEPS - 8 :, :],
        dst_ref=before,
        send_sem=psem.at[0],
        recv_sem=psem.at[1],
        device_id=block(jnp.minimum(place + 1, 127)),
        device_id_type=MESH,
    )

    def to_root(s):
        return pltpu.make_async_remote_copy(
            src_ref=own.at[s],
            dst_ref=ymaps.at[y],
            send_sem=ysend.at[s],
            recv_sem=yrecv.at[y],
            device_id=device(x, c, z, root_at[s]),
            device_id_type=MESH,
        )

    def landed(buffer, sem):
        return pltpu.make_async_remote_copy(
            src_ref=buffer,
            dst_ref=buffer,
            send_sem=sem,
            recv_sem=sem,
            device_id=device(x, c, z, (y + 1) % 4),
            device_id_type=MESH,
        )

    one, none = jnp.int32(1), jnp.int32(0)
    sends = jnp.where(place < 127, one, none) + jnp.where(yroot, 4 * one, 2 * one)
    sends = sends + jnp.where(below, one, none) + jnp.where(zroot, 15 * one, none)
    sends = sends + jnp.where(zroot0, one, none) + jnp.where(zroot1 & (x == 0), 2 * one, none)
    sends = sends + jnp.where(zroot & inner_slab, one, none)
    sends = sends + jnp.where(zroot1 & inner_slab, one, none)
    late = (z == 3) & (y == 3)

    def greeted():
        pl.semaphore_wait(barrier, sends)

        @pl.when(place < 127)
        def _():
            tail.start()

    @pl.when(late)
    def _():
        greeted()

    chains(0, SUB // 2)

    @pl.when(jnp.logical_not(late))
    def _():
        greeted()

    chains(SUB // 2, SUB)

    @pl.when(place > 0)
    def _():
        tail.wait_recv()
        for t in range(2):
            prev[t, 7:8, :] = before[t, 7:8, :]

    @pl.when(place == 0)
    def _():
        for t in range(2):
            prev[t, 7:8, :] = initial[t : t + 1, :]

    earlier = jnp.concatenate([prev[t, 7:15, :] for t in range(2)], axis=0)
    wanted = jnp.concatenate([pre[t * STEPS : t * STEPS + 8, :] for t in range(2)], axis=0)
    steep, added = slopes(earlier, wanted)
    for t in range(2):
        rows = slice(t * 8, t * 8 + 8)
        keep_slopes(slice(t * STEPS, t * STEPS + 8), steep[rows], added[rows])

    for s in range(2):
        of_step(start.at[s], s * STEPS)
        compose(third.at[s], part.at[s, 2], part.at[s, 3])
        compose(first.at[s], start.at[s], part.at[s, 0])
    for s in range(2):
        compose(second.at[s], first.at[s], part.at[s, 1])
    for s in range(2):
        compose(own.at[s], second.at[s], third.at[s])
    for s in range(2):

        @pl.when(root_at[s] != y)
        def _():
            to_root(s).start()

    to_zroot = pltpu.make_async_remote_copy(
        src_ref=ywhole.at[3],
        dst_ref=zmaps.at[z],
        send_sem=zsend,
        recv_sem=zrecv.at[z],
        device_id=device(x, c, ZROOT, y),
        device_id_type=MESH,
    )

    @pl.when(yroot)
    def _():
        ymaps[y] = own[mine]
        for k in (2, 3, 0, 1):

            @pl.when(y != k)
            def _():
                landed(ymaps.at[k], yrecv.at[k]).wait_recv()

            if k == 3:
                compose(ywhole.at[0], ymaps.at[2], ymaps.at[3])
        compose(ywhole.at[1], ymaps.at[0], ymaps.at[1])
        compose(ywhole.at[3], ywhole.at[1], ywhole.at[0])

    @pl.when(below)
    def _():
        to_zroot.start()

    def prefix_out(k):
        return pltpu.make_async_remote_copy(
            src_ref=ymaps.at[0] if k == 1 else ywhole.at[k - 1],
            dst_ref=pmaps.at[mine],
            send_sem=fsend.at[k],
            recv_sem=frecv.at[mine],
            device_id=device(x, c, z, k),
            device_id_type=MESH,
        )

    @pl.when(yroot)
    def _():
        compose(ywhole.at[2], ywhole.at[1], ymaps.at[2])
        for k in range(1, 4):

            @pl.when(y != k)
            def _():
                prefix_out(k).start()

    across = pltpu.make_async_remote_copy(
        src_ref=zwhole.at[3],
        dst_ref=half,
        send_sem=hsem.at[0],
        recv_sem=hsem.at[1],
        device_id=zroot_id(x, 1),
        device_id_type=MESH,
    )
    back = pltpu.make_async_remote_copy(
        src_ref=zwhole.at[3],
        dst_ref=half,
        send_sem=hsem.at[0],
        recv_sem=hsem.at[1],
        device_id=zroot_id(x, 0),
        device_id_type=MESH,
    )
    across0 = pltpu.make_async_remote_copy(
        src_ref=cout,
        dst_ref=cin,
        send_sem=csem.at[0],
        recv_sem=csem.at[1],
        device_id=zroot_id(x, 1),
        device_id_type=MESH,
    )

    def onward(core):
        return pltpu.make_async_remote_copy(
            src_ref=xout,
            dst_ref=xin,
            send_sem=xsend.at[core],
            recv_sem=xrecv,
            device_id=zroot_id(jnp.minimum(x + 1, 3), core),
            device_id_type=MESH,
        )

    def entry_out(k, at):
        return pltpu.make_async_remote_copy(
            src_ref=zout.at[k],
            dst_ref=fin.at[mine],
            send_sem=esend.at[k * 4 + at],
            recv_sem=erecv.at[mine],
            device_id=device(x, c, k, at),
            device_id_type=MESH,
        )

    def zprefix(k):
        return zmaps.at[0] if k == 0 else zwhole.at[k]

    @pl.when(zroot)
    def _():
        for k in (2, 0, 1):
            landed(zmaps.at[k], zrecv.at[k]).wait_recv()
            if k == 2:
                compose(zwhole.at[0], zmaps.at[2], ywhole.at[3])
        compose(zwhole.at[1], zmaps.at[0], zmaps.at[1])
        compose(zwhole.at[3], zwhole.at[1], zwhole.at[0])

        @pl.when((c == 0) & (x == 0))
        def _():
            given = initial[pl.ds(mine, 1), :]
            ein[...] = tile(given)
            cout[...] = tile(applied(as_columns(given), zwhole.at[3]))
            across0.start()
            compose(zwhole.at[2], zwhole.at[1], zmaps.at[2])

        @pl.when((c == 0) & (x > 0))
        def _():
            across.start()
            compose(zwhole.at[2], zwhole.at[1], zmaps.at[2])

            @pl.when(x < 3)
            def _():
                landed(half, hsem.at[1]).wait_recv()
                compose(whole, zwhole.at[3], half)

            landed(xin, xrecv).wait_recv()
            ein[...] = xin[...]

            @pl.when(x < 3)
            def _():
                xout[...] = tile(applied(as_columns(xin[0:1, :]), whole))
                onward(0).start()


        @pl.when((c == 1) & (x == 0))
        def _():
            compose(zwhole.at[2], zwhole.at[1], zmaps.at[2])
            across0.wait_recv()
            ein[...] = cin[...]
            xout[...] = tile(applied(as_columns(cin[0:1, :]), zwhole.at[3]))
            for core in (0, 1):
                onward(core).start()

        @pl.when((c == 1) & (x > 0))
        def _():
            @pl.when(x < 3)
            def _():
                back.start()

            compose(zwhole.at[2], zwhole.at[1], zmaps.at[2])
            across.wait_recv()

            @pl.when(x == 2)
            def _():
                compose(whole, half, zwhole.at[3])

            landed(xin, xrecv).wait_recv()
            columns = as_columns(xin[0:1, :])

            @pl.when(x == 2)
            def _():
                xout[...] = tile(applied(columns, whole))
                onward(1).start()

            ein[...] = tile(applied(columns, half))

            @pl.when(x == 1)
            def _():
                xout[...] = tile(applied(as_columns(ein[0:1, :]), zwhole.at[3]))
                onward(1).start()

        columns = as_columns(ein[0:1, :])
        for k in range(4):
            zout[k] = ein[...] if k == 0 else tile(applied(columns, zprefix(k - 1)))
            for at in range(4):
                if k != ZROOT:
                    entry_out(k, at).start()
                else:

                    @pl.when(y != at)
                    def _():
                        entry_out(k, at).start()

        fin[mine] = zout[ZROOT]

    for s in range(2):

        @pl.when((y > 0) & (root_at[s] != y))
        def _():
            landed(pmaps.at[s], frecv.at[s]).wait_recv()

    @pl.when(yroot & (y == 1))
    def _():
        pmaps[mine] = ymaps[0]

    for k in range(2, 4):

        @pl.when(yroot & (y == k))
        def _():
            pmaps[mine] = ywhole[k - 1]

    for s in range(2):

        @pl.when(jnp.logical_not(zroot & (mine == s)))
        def _():
            landed(fin.at[s], erecv.at[s]).wait_recv()

    entries[...] = fin[...]

    @pl.when(y > 0)
    def _():
        for s in range(2):
            entries[s] = tile(applied(as_columns(fin[s, 0:1, :]), pmaps.at[s]))

    for s in range(2):
        entry = entries[s, 0:1, :]
        columns = as_columns(entry)
        middle = applied(columns, second.at[s])
        at = s * SUBS
        state[at : at + 1, :] = entry
        state[at + 1 : at + 2, :] = applied(columns, first.at[s])
        state[at + 2 : at + 3, :] = middle
        state[at + 3 : at + 4, :] = applied(as_columns(middle), part.at[s, 2])
    now = state[...]
    for inner in range(SUB):
        turned = dot3(now, skew_hi[...], skew_lo[...])
        at = pl.ds(inner, 2 * SUBS, stride=SUB)
        steep = jnp.concatenate([slope2[lanes, at, :] for lanes in range(2)], axis=1)
        added = jnp.concatenate([offset2[lanes, at, :] for lanes in range(2)], axis=1)
        now = keep * now + steep * turned + added
        for lanes in range(2):
            out2[lanes, at, :] = now[:, lanes * 128 : lanes * 128 + 128]
    for lanes in range(2):
        out[:, lanes * 128 : lanes * 128 + 128] = out2[lanes]

    @pl.when(place < 127)
    def _():
        tail.wait_send()

    for s in range(2):

        @pl.when(root_at[s] != y)
        def _():
            to_root(s).wait_send()

    @pl.when(below)
    def _():
        to_zroot.wait_send()

    @pl.when(zroot0 & (x == 0))
    def _():
        across0.wait_send()

    @pl.when(zroot0 & (x > 0))
    def _():
        across.wait_send()

    @pl.when(zroot1 & inner_slab)
    def _():
        back.wait_send()

    @pl.when(zroot1 & (x < 3))
    def _():
        onward(1).wait_send()

    @pl.when((zroot1 & (x == 0)) | (zroot0 & inner_slab))
    def _():
        onward(0).wait_send()

    @pl.when(zroot)
    def _():
        for k in range(4):
            for at in range(4):
                if k != ZROOT:
                    entry_out(k, at).wait_send()
                else:

                    @pl.when(y != at)
                    def _():
                        entry_out(k, at).wait_send()

    @pl.when(yroot)
    def _():
        for k in range(1, 4):

            @pl.when(y != k)
            def _():
                prefix_out(k).wait_send()


def per_device(guess, inputs, initial, skew_base, in_weight, bias, rate):
    dma = pltpu.SemaphoreType.DMA

    def f32(*shape):
        return pltpu.VMEM(shape, F32)

    maps = (ROWS, WIDTH)
    states = pl.pallas_call(
        kernel,
        out_shape=jax.ShapeDtypeStruct((2 * STEPS, WIDTH), F32),
        in_specs=[pl.BlockSpec(memory_space=pltpu.HBM)] * 7,
        out_specs=pl.BlockSpec(memory_space=pltpu.VMEM),
        scratch_shapes=[
            f32(2, STEPS, WIDTH),
            pltpu.VMEM((2, STEPS, WIDTH), BF16),
            f32(2, WIDTH),
            f32(WIDTH, WIDTH),
            pltpu.VMEM((WIDTH, WIDTH), BF16),
            f32(1, WIDTH),
            f32(1, WIDTH),
            f32(WIDTH, WIDTH),
            pltpu.VMEM((WIDTH, WIDTH), BF16),
            pltpu.VMEM((WIDTH, WIDTH), BF16),
            f32(WIDTH, WIDTH),
            f32(2, 8, WIDTH),
            f32(2, STEPS + 8, WIDTH),
            f32(2 * STEPS, WIDTH),
            f32(2 * STEPS, WIDTH),
            f32(2 * STEPS, WIDTH),
            f32(2, 2 * STEPS, 128),
            f32(2, 2 * STEPS, 128),
            f32(2, 2 * STEPS, 128),
            f32(2, SUBS, *maps),
            f32(2, *maps),
            f32(2, *maps),
            f32(2, *maps),
            f32(2, *maps),
            f32(2, *maps),
            f32(4, *maps),
            f32(4, *maps),
            f32(4, *maps),
            f32(4, *maps),
            f32(*maps),
            f32(*maps),
            f32(2, *maps),
            f32(8, WIDTH),
            f32(8, WIDTH),
            f32(8, WIDTH),
            f32(8, WIDTH),
            f32(8, WIDTH),
            f32(4, 8, WIDTH),
            f32(2, 8, WIDTH),
            f32(2, 8, WIDTH),
            f32(8, WIDTH),
            dma((7,)),
            dma((2,)),
            dma((2,)),
            dma((4,)),
            dma,
            dma((4,)),
            dma((2,)),
            dma((2,)),
            dma((2,)),
            dma,
            dma((16,)),
            dma((2,)),
            dma((4,)),
            dma((2,)),
        ],
        compiler_params=pltpu.CompilerParams(
            collective_id=0, has_side_effects=True, vmem_limit_bytes=60 * 1024 * 1024
        ),
    )(
        guess,
        inputs,
        initial,
        skew_base,
        in_weight,
        bias.reshape(1, WIDTH),
        rate.reshape(1, WIDTH),
    )
    return states.reshape(2, STEPS, WIDTH)


def solution(mesh):
    return jax.shard_map(
        per_device,
        mesh=mesh,
        in_specs=(P(None, SEQ_GRP, None), P(None, SEQ_GRP, None), P(), P(), P(), P(), P()),
        out_specs=P(None, SEQ_GRP, None),
        check_vma=False,
    )
```
